512 devices in a mesh: rows: 128 (over z_hi, x, y), rep: 4 (over z_lo, core).
Axes of the slice: x: 4, y: 8, z: 8 (z_hi: 4, z_lo: 2; z = z_hi * 2 + z_lo), core: 2. Of those that a mesh axis runs over, the one named last changes fastest.
Arguments:
- features: bfloat16 [16384, 128], P('rows', 'rep'), may hold values from -6 to 6
- weight: bfloat16 [128, 128], replicated, may hold values from -0.5 to 0.5
- tiles: bfloat16 [128, 16, 128, 128], P('rows'), may hold values from -0.1875 to 0.1875
- tile_rows: int32 [128, 16], P('rows'), may hold values from 0 to 127
- tile_live: int32 [128, 16], P('rows'), may hold values from 0 to 1, as said below
- pos_partner: int32 [16384, 8], P('rows'), may hold values from 0 to 16383
- neg_partner: int32 [16384, 8], P('rows'), may hold values from 0 to 16383
Outputs:
- embedding: bfloat16 [16384, 128], P('rows', 'rep')
- grad_weight: float32 [128, 128], P('rep')
- grad_features: bfloat16 [16384, 128], P('rows', 'rep')
The draws below stay inside these ranges and needn't reach their ends.
Inputs may be any that keep to these rules, and one draw needn't show every extreme that they name: `tile_live`: the share of live slots differs between column blocks.
All inputs are finite; a program needn't handle non-finite values.
Results may differ from the reference program's by a relative error of at most 0.008.
Values may be sent and summed in bfloat16 or wider, within the bound.
No kernel may reach another device: no remote copies, remote signals or barrier semaphores. Data moves between devices by JAX's collectives and lax.ppermute only.
A program may use at most 64 MiB of HBM per device.

```python
import math
import jax
import jax.numpy as jnp
from jax import lax

F = 128
BLOCK = 128
KSLOT = 16
PK = 8
NBLK = 128
NODES = 16384


def draw_tile_live(key, part):
    key = jax.random.fold_in(key, 11)
    level_key, slot_key = jax.random.split(key)
    exponents = jax.random.randint(level_key, (NBLK, 1), 0, 4)
    levels = jnp.left_shift(jnp.ones((NBLK, 1), jnp.int32), exponents)
    slot_picks = jax.random.randint(slot_key, (NBLK, KSLOT), 0, 8)
    return (slot_picks < levels).astype(jnp.int32)


def touch_ends(values, own_key, low, high):
    dims = values.shape
    index_at = [jax.random.randint(jax.random.fold_in(own_key, axis), (), 0, dims[axis]) for axis in range(len(dims))]
    values = values.at[tuple(index_at)].set(low)
    longest = dims.index(max(dims))
    index_at[longest] = (index_at[longest] + 1) % dims[longest]
    return values.at[tuple(index_at)].set(high)


def block_levels(rng, shape, cuts, low, top_value):
    gain, own = 1.0, jax.random.fold_in(rng, 6)
    for axis_at, parts in cuts:
        steps = jnp.exp(jax.random.uniform(jax.random.fold_in(own, axis_at), (parts,), jnp.float32, low / len(cuts), top_value / len(cuts)))
        gain = gain * jnp.repeat(steps, shape[axis_at] // parts).reshape([-1 if axis == axis_at else 1 for axis in range(len(shape))])
    return gain


def noise(stream_key, dims, scale, reach, cuts=(), dtype=jnp.bfloat16):
    factor_of = block_levels(stream_key, dims, cuts, -0.22, 0.18) if cuts else 1.0
    entries = jax.random.normal(stream_key, dims, jnp.float32) * scale * factor_of
    return jnp.minimum(jnp.maximum(entries, -reach), reach).astype(dtype)


def setup_inputs(seed: int = 0) -> dict:
    seeds = jax.random.split(jax.random.key(seed), 8)
    features = noise(seeds[0], (NODES, F), 1.0, 6.0, ((0, 128), (1, 4)))
    weight = noise(seeds[1], (F, F), F ** -0.5, 0.5)
    tiles = noise(seeds[2], (NBLK, KSLOT, BLOCK, BLOCK), (BLOCK * KSLOT // 2) ** -0.5, 0.1875, ((0, 128),))
    tile_rows = touch_ends(jax.random.randint(seeds[3], (NBLK, KSLOT), 0, NBLK), jax.random.fold_in(seeds[3], 1), 0, NBLK - 1).astype(jnp.int32)
    tile_live = draw_tile_live(jax.random.fold_in(seeds[7], 71), 0)
    pos_partner = touch_ends(jax.random.randint(seeds[5], (NODES, PK), 0, NODES), jax.random.fold_in(seeds[5], 1), 0, NODES - 1).astype(jnp.int32)
    neg_partner = touch_ends(jax.random.randint(seeds[6], (NODES, PK), 0, NODES), jax.random.fold_in(seeds[6], 1), 0, NODES - 1).astype(jnp.int32)
    return {"features": features, "weight": weight, "tiles": tiles, "tile_rows": tile_rows, "tile_live": tile_live, "pos_partner": pos_partner, "neg_partner": neg_partner}


def pair_grads(embedding, partners, target_label):
    wide_embed = embedding.astype(jnp.float32)
    partner_rows = wide_embed[partners]
    logits = jnp.einsum('nf,nkf->nk', wide_embed, partner_rows, precision=lax.Precision.HIGHEST) / math.sqrt(F)
    coeffs = (jax.nn.sigmoid(logits) - target_label) / PK
    direct = jnp.einsum('nk,nkf->nf', coeffs, partner_rows, precision=lax.Precision.HIGHEST)
    pair_terms = coeffs[:, :, None] * wide_embed[:, None, :]
    incoming = jnp.zeros((NODES, F), jnp.float32).at[partners.reshape(-1)].add(pair_terms.reshape(-1, F))
    return direct + incoming

def reference(features, weight, tiles, tile_rows, tile_live, pos_partner, neg_partner):
    live_flags = tile_live.astype(jnp.float32)
    panels = features.reshape(NBLK, BLOCK, F)

    def column(running, inputs):
        blocks, row_ids, flags_now, panel_now = inputs
        products = jnp.einsum('kij,jf->kif', blocks.astype(jnp.float32), panel_now.astype(jnp.float32))
        return (running.at[row_ids].add(products * flags_now[:, None, None]), None)
    start_total = jnp.zeros((NBLK, BLOCK, F), jnp.float32)
    summed, _ = lax.scan(column, start_total, (tiles, tile_rows, live_flags, panels))
    rounded_agg = summed.reshape(NODES, F).astype(jnp.bfloat16)
    embedding = jnp.dot(rounded_agg, weight, preferred_element_type=jnp.float32).astype(jnp.bfloat16)
    grad_embed = pair_grads(embedding, pos_partner, 1.0) + pair_grads(embedding, neg_partner, 0.0)
    grad_rounded = grad_embed.astype(jnp.bfloat16)
    grad_weight = jnp.dot(rounded_agg.T, grad_rounded, preferred_element_type=jnp.float32) / math.sqrt(NODES)
    grad_agg = jnp.dot(grad_rounded, weight.T, preferred_element_type=jnp.float32).astype(jnp.bfloat16)
    grad_blocks = grad_agg.reshape(NBLK, BLOCK, F)

    def transpose_column(running, inputs):
        blocks, row_ids, flags_now = inputs
        selected = grad_blocks[row_ids].astype(jnp.float32) * flags_now[:, None, None]
        return (running, jnp.einsum('kij,kif->jf', blocks.astype(jnp.float32), selected))
    _, column_grads = lax.scan(transpose_column, jnp.float32(0.0), (tiles, tile_rows, live_flags))
    grad_features = column_grads.reshape(NODES, F).astype(jnp.bfloat16)
    return (embedding, grad_weight, grad_features)
```

```python
import functools
import math

import jax
import jax.numpy as jnp
from jax import lax
from jax.experimental import pallas as pl
from jax.experimental.pallas import tpu as pltpu
from jax.sharding import Mesh, PartitionSpec as P

BF = jnp.bfloat16
F32 = jnp.float32
B = 128
F = 128
W32 = 32
ROWS = ("zh", "x", "y")
REP = ("zl", "core")
PARAMS = pltpu.CompilerParams(vmem_limit_bytes=40 * 1024 * 1024)
VMEM = pl.BlockSpec(memory_space=pltpu.VMEM)
SMEM = pl.BlockSpec(memory_space=pltpu.SMEM)


def tn(a, b):
    return lax.dot_general(a, b, (((0,), (0,)), ((), ())), preferred_element_type=F32)


def nt(a, b):
    return lax.dot_general(a, b, (((1,), (1,)), ((), ())), preferred_element_type=F32)


def nn(a, b):
    return lax.dot_general(a, b, (((1,), (0,)), ((), ())), preferred_element_type=F32)


def call(body, in_specs, out_shape, scratch=(), flops=1000000, nbytes=1000000):
    multi = isinstance(out_shape, (tuple, list))
    return pl.pallas_call(
        body,
        out_shape=out_shape,
        in_specs=in_specs,
        out_specs=[VMEM] * len(out_shape) if multi else VMEM,
        scratch_shapes=list(scratch),
        compiler_params=PARAMS,
        cost_estimate=pl.CostEstimate(flops=flops, bytes_accessed=nbytes, transcendentals=0),
    )


def products_kernel(xy, rows_ref, live_ref, feat_ref, tiles_ref, out_ref, acc):
    acc[...] = jnp.zeros_like(acc)
    slots = tiles_ref.shape[1]
    for s in range(slots):
        prod = nt(feat_ref[...], tiles_ref[0, s]) * live_ref[0, s].astype(F32)
        row = rows_ref[0, s]
        acc[lax.rem(row, xy), lax.div(row, xy)] += prod
    out_ref[...] = acc[...].astype(BF)


def direct_kernel(xy, place_ref, pos_ref, neg_ref, cpos_ref, ctot_ref, ids):
    pk = pos_ref.shape[1]
    for k in range(pk):
        ids[k] = jnp.broadcast_to(pos_ref[:, k : k + 1], (B, B))
        ids[pk + k] = jnp.broadcast_to(neg_ref[:, k : k + 1], (B, B))
    lane = lax.broadcasted_iota(jnp.int32, (B, B), 1)
    base = place_ref[0] * xy * B

    def step(mb, carry):
        want = lane + (base + mb * B)
        cpos = jnp.zeros((B, B), F32)
        cneg = jnp.zeros((B, B), F32)
        for k in range(pk):
            cpos = jnp.where(ids[k] == want, cpos + 1.0, cpos)
            cneg = jnp.where(ids[pk + k] == want, cneg + 1.0, cneg)
        cpos_ref[mb] = cpos.astype(BF)
        ctot_ref[mb] = (cpos + cneg).astype(BF)
        return carry

    lax.fori_loop(0, xy, step, 0)


def partial_kernel(recv_ref, pos_ref, neg_ref, out_ref):
    out_ref[0:B, :] = jnp.sum(recv_ref[...].astype(F32), axis=0).astype(BF)
    pk = pos_ref.shape[0]
    table = jnp.concatenate([pos_ref[...], neg_ref[...]], axis=0)
    block = lax.shift_right_logical(table, 7)
    out_ref[B : B + 2 * pk, :] = block.astype(F32).astype(BF)
    out_ref[B + 2 * pk :, :] = (table - block * B).astype(F32).astype(BF)


def embed_kernel(q, place_ref, got_ref, w_ref, eown_ref, embt_ref, aggt_ref, send_ref, agg_s, et_s):
    part, plane = place_ref[0], place_ref[1]

    def block_agg(b):
        first = pl.multiple_of(b * W32, W32)
        for p in range(q):
            total = got_ref[p, pl.ds(first, W32), :].astype(F32)
            for z in range(1, q):
                total = total + got_ref[z * q + p, pl.ds(first, W32), :].astype(F32)
            agg_s[p * W32 : (p + 1) * W32, :] = total.astype(BF)

    mine = pl.ds(pl.multiple_of(part * W32, W32), W32)
    block_agg(part)
    send = tn(agg_s[...], w_ref[...]).astype(BF)
    table = got_ref[part * q, B:, :]
    for d in range(send_ref.shape[0]):
        send_ref[d, 0:B, :] = send
        send_ref[d, B:, :] = table
    block_agg(plane)
    et = tn(w_ref[...], agg_s[...])
    et_s[...] = et.astype(BF)
    eown_ref[...] = et.T.astype(BF)
    embt_ref[...] = et_s[mine, :]
    aggt_ref[...] = agg_s[mine, :]


def decoder_kernel(group, place_ref, got_ref, eown_ref, cpos_ref, ctot_ref, out_ref):
    blocks = got_ref.shape[0]
    slots = (got_ref.shape[1] - B) // 2
    pk = slots // 2
    own = place_ref[2].astype(F32)
    sub = lax.broadcasted_iota(jnp.int32, (B, B), 0).astype(F32)
    eown = eown_ref[...]
    scale = 1.0 / math.sqrt(F)

    def step(i, acc):
        terms = []
        first = i * group
        em = got_ref[pl.ds(first, group), 0:B, :].reshape(group * B, F)
        logits = nt(eown, em)
        for j in range(group):
            mb = first + j
            tab = got_ref[mb, B:, :].astype(F32)
            place = jnp.where(tab[:slots] == own, tab[slots:], -1.0)
            cpos = cpos_ref[mb].astype(F32)
            ctot = ctot_ref[mb].astype(F32)
            ipos = jnp.zeros((B, B), F32)
            ineg = jnp.zeros((B, B), F32)
            for k in range(pk):
                ipos = jnp.where(sub == place[k : k + 1], ipos + 1.0, ipos)
                ineg = jnp.where(sub == place[pk + k : pk + k + 1], ineg + 1.0, ineg)
            sig = jax.nn.sigmoid(logits[:, j * B : (j + 1) * B] * scale)
            coef = (ctot + ipos + ineg) * sig - (cpos + ipos)
            terms.append(coef)
        coefs = jnp.concatenate(terms, axis=1)
        high = coefs.astype(BF)
        low = (coefs - high.astype(F32)).astype(BF)
        return acc + nn(high, em) + nn(low, em)

    acc = lax.fori_loop(0, blocks // group, step, jnp.zeros((B, F), F32))
    out_ref[...] = acc * (1.0 / pk)


def grads_kernel(q, place_ref, got_ref, w_ref, aggt_ref, out_ref):
    total = got_ref[0:B, :]
    for p in range(1, q):
        total = total + got_ref[p * B : (p + 1) * B, :]
    grad = total.astype(BF)
    wrows = w_ref[pl.ds(pl.multiple_of(place_ref[0] * W32, W32), W32), :]
    grad_agg = nt(wrows, grad).astype(BF)
    terms = nn(aggt_ref[...], grad)
    high = terms.astype(BF)
    low = (terms - high.astype(F32)).astype(BF)
    for d in range(out_ref.shape[0]):
        out_ref[d, 0:W32, :] = grad_agg
        out_ref[d, W32 : 2 * W32, :] = high
        out_ref[d, 2 * W32 :, :] = low


def merge_kernel(got_ref, out_ref):
    ny = got_ref.shape[0]
    terms = jnp.sum(
        got_ref[:, W32 : 2 * W32, :].astype(F32) + got_ref[:, 2 * W32 :, :].astype(F32), axis=0
    )
    high = terms.astype(BF)
    low = (terms - high.astype(F32)).astype(BF)
    blocks = got_ref[:, 0:W32, :].reshape(ny * W32, B)
    for d in range(out_ref.shape[0]):
        out_ref[d, 0 : ny * W32, :] = blocks
        out_ref[d, ny * W32 : (ny + 1) * W32, :] = high
        out_ref[d, (ny + 1) * W32 :, :] = low


def features_kernel(ny, node_count, rows_ref, live_ref, got_ref, tiles_ref, gft_ref, gw_ref):
    slots = tiles_ref.shape[1]
    total = jnp.zeros((W32, B), F32)
    for s in range(slots):
        row = rows_ref[0, s]
        first = pl.multiple_of(lax.rem(row, ny) * W32, W32)
        block = got_ref[lax.div(row, ny), pl.ds(first, W32), :]
        block = (block.astype(F32) * live_ref[0, s].astype(F32)).astype(BF)
        total = total + nn(block, tiles_ref[0, s])
    gft_ref[...] = total.astype(BF)
    first = ny * W32
    terms = got_ref[:, first : first + W32, :].astype(F32) + got_ref[:, first + W32 :, :].astype(F32)
    gw_ref[...] = jnp.sum(terms, axis=0) * (1.0 / math.sqrt(node_count))


def on_device(features, weight, tiles, tile_rows, tile_live, pos_partner, neg_partner):
    q = lax.axis_size("zh")
    nx, ny = lax.axis_size("x"), lax.axis_size("y")
    xy = nx * ny
    node_count = q * xy * B
    plane, part = lax.axis_index("zh"), lax.axis_index(REP)
    own_block = lax.axis_index(ROWS)
    place = jnp.stack([part, plane, own_block]).astype(jnp.int32)
    shape = jax.ShapeDtypeStruct
    pos_t, neg_t = pos_partner.T, neg_partner.T
    slots = 2 * pos_partner.shape[1]

    sent = call(
        functools.partial(products_kernel, xy),
        [SMEM, SMEM, VMEM, VMEM],
        shape((xy, q, W32, B), BF),
        [pltpu.VMEM((xy, q, W32, B), F32)],
    )(tile_rows, tile_live, features.T, tiles)
    recv = lax.all_to_all(sent.reshape(xy, q * W32, B), ("x", "y"), 0, 0, tiled=True)

    cpos, ctot = call(
        functools.partial(direct_kernel, xy),
        [SMEM, VMEM, VMEM],
        (shape((xy, B, B), BF), shape((xy, B, B), BF)),
        [pltpu.VMEM((slots, B, B), jnp.int32)],
        flops=100000000,
    )(place, pos_partner, neg_partner)

    partial_value = call(partial_kernel, [VMEM, VMEM, VMEM], shape((q * W32 + 2 * slots, B), BF))(
        recv, pos_t, neg_t
    )
    height = partial_value.shape[0]
    gathered = lax.all_gather(partial_value, ("zh",) + REP, axis=0)

    eown, emb_t, agg_t, slab_part = call(
        functools.partial(embed_kernel, q),
        [SMEM, VMEM, VMEM],
        (shape((B, F), BF), shape((W32, B), BF), shape((W32, B), BF), shape((xy, height, B), BF)),
        [pltpu.VMEM((F, B), BF), pltpu.VMEM((F, B), BF)],
    )(place, gathered, weight)
    slab = lax.all_to_all(slab_part, ("x", "y"), 0, 0, tiled=True)

    group = math.gcd(xy, 4)
    grad_part = call(
        functools.partial(decoder_kernel, group),
        [SMEM, VMEM, VMEM, VMEM, VMEM],
        shape((B, F), F32),
    )(place, slab, eown, cpos, ctot)
    grad_parts = lax.all_gather(grad_part, REP, axis=0, tiled=True)

    line_part = call(
        functools.partial(grads_kernel, q),
        [SMEM, VMEM, VMEM, VMEM],
        shape((ny, 3 * W32, B), BF),
    )(place, grad_parts, weight, agg_t)
    line = lax.all_to_all(line_part, "y", 0, 0, tiled=True)
    rest_part = call(merge_kernel, [VMEM], shape((q * nx, (ny + 2) * W32, B), BF))(line)
    rest = lax.all_to_all(rest_part, ("zh", "x"), 0, 0, tiled=True)

    gf_t, grad_weight = call(
        functools.partial(features_kernel, ny, node_count),
        [SMEM, SMEM, VMEM, VMEM],
        (shape((W32, B), BF), shape((W32, F), F32)),
    )(tile_rows, tile_live, rest, tiles)
    return (emb_t.T, grad_weight, gf_t.T)


def sharded(mesh):
    return jax.shard_map(
        on_device,
        mesh=mesh,
        in_specs=(
            P(ROWS, REP),
            P(),
            P(ROWS, None, None, None),
            P(ROWS, None),
            P(ROWS, None),
            P(ROWS, None),
            P(ROWS, None),
        ),
        out_specs=(P(ROWS, REP), P(REP, None), P(ROWS, REP)),
        check_vma=False,
    )


def solution(mesh):
    rows = mesh.shape["rows"]
    parts = mesh.devices.reshape(4, 4, rows // 16, 2, 2)
    return sharded(Mesh(parts, ("zh", "x", "y", "zl", "core")))
```

```python
import functools
import math

import jax
import jax.numpy as jnp
from jax import lax
from jax.experimental import pallas as pl
from jax.experimental.pallas import tpu as pltpu
from jax.sharding import Mesh, PartitionSpec as P

BF = jnp.bfloat16
F32 = jnp.float32
B = 128
F = 128
W32 = 32
ROWS = ("zh", "x", "y")
REP = ("zl", "core")
PARAMS = pltpu.CompilerParams(vmem_limit_bytes=40 * 1024 * 1024)
VMEM = pl.BlockSpec(memory_space=pltpu.VMEM)
SMEM = pl.BlockSpec(memory_space=pltpu.SMEM)


def tn(a, b):
    return lax.dot_general(a, b, (((0,), (0,)), ((), ())), preferred_element_type=F32)


def nt(a, b):
    return lax.dot_general(a, b, (((1,), (1,)), ((), ())), preferred_element_type=F32)


def nn(a, b):
    return lax.dot_general(a, b, (((1,), (0,)), ((), ())), preferred_element_type=F32)


def call(body, in_specs, out_shape, scratch=(), flops=1000000, nbytes=1000000):
    multi = isinstance(out_shape, (tuple, list))
    return pl.pallas_call(
        body,
        out_shape=out_shape,
        in_specs=in_specs,
        out_specs=[VMEM] * len(out_shape) if multi else VMEM,
        scratch_shapes=list(scratch),
        compiler_params=PARAMS,
        cost_estimate=pl.CostEstimate(flops=flops, bytes_accessed=nbytes, transcendentals=0),
    )


def split(value):
    high = value.astype(BF).astype(F32)
    return high, value - high


def products_kernel(rows_ref, live_ref, feat_ref, tiles_ref, out_ref, acc):
    acc[...] = jnp.zeros_like(acc)
    for s in range(tiles_ref.shape[1]):
        prod = nt(feat_ref[...], tiles_ref[0, s]) * live_ref[0, s].astype(F32)
        acc[rows_ref[0, s]] += prod
    out_ref[...] = acc[...].astype(BF)


def aggregate_kernel(place_ref, recv_ref, pos_ref, neg_ref, out_ref):
    part = place_ref[0]
    total = recv_ref[0].astype(F32)
    for r in range(1, recv_ref.shape[0]):
        total = total + recv_ref[r].astype(F32)
    table = jnp.concatenate([pos_ref[...], neg_ref[...]], axis=0)
    block = lax.shift_right_logical(table, 7)
    sent = jnp.where(part == 0, block, table - block * B).astype(F32).astype(BF)
    total = total.astype(BF)
    for d in range(out_ref.shape[0]):
        out_ref[d, 0:W32, :] = total
        out_ref[d, W32:, :] = sent


def embed_kernel(q, place_ref, got_ref, w_ref, enodes_ref, agg_ref, embt_ref, send_ref, et_s, piece_s):
    part, plane = place_ref[0], place_ref[1]
    slots = got_ref.shape[1] - W32
    for b in range(q):
        for p in range(q):
            agg_ref[b, p * W32 : (p + 1) * W32, :] = got_ref[b * q + p, 0:W32, :]
        et = tn(w_ref[...], agg_ref[b])
        et_s[b] = et.astype(BF)
        enodes_ref[b * B : (b + 1) * B, :] = et.T.astype(BF)
    mine = pl.ds(pl.multiple_of(part * W32, W32), W32)
    embt_ref[...] = et_s[plane, mine, :]
    blocks = got_ref[part * q, W32:, :].astype(F32)
    places = got_ref[part * q + 1, W32:, :].astype(F32)
    table = jnp.concatenate([blocks, places, jnp.zeros((B - 2 * slots, B), F32)], axis=0)
    piece_s[...] = table.T.astype(BF)
    rows = pl.multiple_of(plane * W32, W32)
    nodes = enodes_ref[pl.ds(pl.multiple_of(part * B + plane * W32, W32), W32), :]
    partners = piece_s[pl.ds(rows, W32), :]
    for d in range(send_ref.shape[0]):
        send_ref[d, 0:W32, :] = nodes
        send_ref[d, W32:, :] = partners


def direct_kernel(q, xy, place_ref, got_ref, cpos_ref, ctot_ref):
    part, plane = place_ref[0], place_ref[1]
    slots = got_ref.shape[1] - W32
    pk = slots // 2
    first_block = (part * xy).astype(F32)
    first_place = (plane * W32).astype(F32)
    sub = lax.broadcasted_iota(jnp.int32, (B, B), 0).astype(F32)
    chunks = cpos_ref.shape[1] // B
    for b in range(q):
        block = got_ref[b * q, W32:, :].astype(F32) - first_block
        place = got_ref[b * q + 1, W32:, :].astype(F32) - first_place
        inside = (block >= 0.0) & (block < float(xy)) & (place >= 0.0) & (place < float(W32))
        want = jnp.where(inside, block * W32 + place, -1.0)

        def step(c, carry):
            at = sub + (c * B).astype(F32)
            cpos = jnp.zeros((B, B), F32)
            cneg = jnp.zeros((B, B), F32)
            for k in range(pk):
                cpos = jnp.where(at == want[k : k + 1], cpos + 1.0, cpos)
                cneg = jnp.where(at == want[pk + k : pk + k + 1], cneg + 1.0, cneg)
            rows = pl.ds(pl.multiple_of(c * B, B), B)
            cpos_ref[b, rows, :] = cpos.astype(BF)
            ctot_ref[b, rows, :] = (cpos + cneg).astype(BF)
            return carry

        lax.fori_loop(0, chunks, step, 0)


def decoder_kernel(
    q, xy, place_ref, got_ref, en_ref, agg_ref, w_ref, cpos_ref, ctot_ref, out_ref,
    em_s, code_s, wide_s, logit_s, high_s, low_s,
):
    slots = wide_s.shape[0]
    pk = slots // 2
    col = place_ref[2]
    pieces = got_ref.shape[0]
    count = pieces * W32
    em_s[...] = got_ref[:, 0:W32, :].reshape(count, F)
    table = got_ref[:, W32:, :].reshape(count, B).astype(F32)
    places = pltpu.roll(table, B - slots, 1)
    code = jnp.full((count, B), -1.0, F32)
    for b in range(q):
        code = jnp.where(table == (b * xy + col).astype(F32), places + float(b * B), code)
    code_s[...] = code
    logit_s[...] = nt(em_s[...], en_ref[...])
    lane = lax.broadcasted_iota(jnp.int32, (B, B), 1).astype(F32)
    scale = 1.0 / math.sqrt(F)

    def step(c, carry):
        rows = pl.ds(pl.multiple_of(c * B, B), B)
        for k in range(slots):
            wide_s[k] = jnp.broadcast_to(code_s[rows, k : k + 1], (B, B))
        for b in range(q):
            at = lane + float(b * B)
            ipos = cpos_ref[b, rows, :].astype(F32)
            itot = ctot_ref[b, rows, :].astype(F32)
            ineg = jnp.zeros((B, B), F32)
            both = jnp.zeros((B, B), F32)
            for k in range(pk):
                both = jnp.where(wide_s[k] == at, both + 1.0, both)
                ineg = jnp.where(wide_s[pk + k] == at, ineg + 1.0, ineg)
            cols = slice(b * B, (b + 1) * B)
            sig = jax.nn.sigmoid(logit_s[rows, cols] * scale)
            coef = (itot + both + ineg) * sig - (ipos + both)
            high, low = split(coef)
            high_s[rows, cols] = high.astype(BF)
            low_s[rows, cols] = low.astype(BF)
        return carry

    lax.fori_loop(0, count // B, step, 0)
    em_t = em_s[...].astype(F32).T.astype(BF)
    grad = (nn(em_t, high_s[...]) + nn(em_t, low_s[...])) * (1.0 / pk)
    high, low = split(grad)
    high, low = high.astype(BF), low.astype(BF)
    grad_agg = nn(w_ref[...], high) + nn(w_ref[...], low)
    terms = jnp.zeros((F, F), F32)
    for b in range(q):
        cols = slice(b * B, (b + 1) * B)
        terms = terms + nt(agg_ref[b], high[:, cols]) + nt(agg_ref[b], low[:, cols])
    thigh, tlow = split(terms)
    eighth = W32 // q
    for z in range(q):
        for p in range(q):
            first = p * W32 + z * eighth
            piece = [
                grad_agg[p * W32 : (p + 1) * W32, z * B : (z + 1) * B],
                thigh[first : first + eighth],
                tlow[first : first + eighth],
            ]
            out_ref[z * q + p] = jnp.concatenate(piece, axis=0).astype(BF)


def owner_kernel(q, got_ref, out_ref):
    total = got_ref[0].astype(F32)
    for r in range(1, got_ref.shape[0]):
        total = total + got_ref[r].astype(F32)
    eighth = W32 // q
    high, low = split(total[W32 : W32 + eighth] + total[W32 + eighth :])
    sent = jnp.concatenate([total[:W32], high, low], axis=0).astype(BF)
    for d in range(out_ref.shape[0]):
        out_ref[d] = sent


def merge_kernel(q, got_ref, out_ref):
    count = got_ref.shape[0]
    ny = count // q
    eighth = W32 // q
    out_ref[0 : count * W32, :] = got_ref[:, 0:W32, :].reshape(count * W32, B)
    rows = []
    for z in range(q):
        total = got_ref[z * ny, W32:, :].astype(F32)
        for y in range(1, ny):
            total = total + got_ref[z * ny + y, W32:, :].astype(F32)
        rows.append(total[:eighth] + total[eighth:])
    high, low = split(jnp.concatenate(rows, axis=0))
    out_ref[count * W32 : (count + 1) * W32, :] = high.astype(BF)
    out_ref[(count + 1) * W32 :, :] = low.astype(BF)


def features_kernel(q, nx, ny, place_ref, rows_ref, live_ref, *refs):
    got, (tiles_ref, gft_ref, gw_ref) = refs[:nx], refs[nx:]
    my_x = place_ref[3]
    total = jnp.zeros((W32, B), F32)
    for s in range(tiles_ref.shape[1]):
        row = rows_ref[0, s]
        plane = lax.div(row, nx * ny)
        line = lax.rem(lax.div(row, ny), nx)
        ahead = lax.rem(my_x - line + nx, nx)
        first = pl.multiple_of((plane * ny + lax.rem(row, ny)) * W32, W32)
        live = live_ref[0, s].astype(F32)
        block = jnp.zeros((W32, B), F32)
        for d in range(nx):
            use = jnp.where(ahead == d, live, 0.0)
            block = block + got[d][pl.ds(first, W32), :].astype(F32) * use
        total = total + nn(block.astype(BF), tiles_ref[0, s])
    gft_ref[...] = total.astype(BF)
    first = q * ny * W32
    terms = jnp.zeros((W32, F), F32)
    for d in range(nx):
        terms = terms + got[d][first : first + W32, :].astype(F32)
        terms = terms + got[d][first + W32 : first + 2 * W32, :].astype(F32)
    gw_ref[...] = terms * (1.0 / math.sqrt(q * nx * ny * B))


def on_device(features, weight, tiles, tile_rows, tile_live, pos_partner, neg_partner):
    q = lax.axis_size("zh")
    nx, ny = lax.axis_size("x"), lax.axis_size("y")
    xy = nx * ny
    plane, part = lax.axis_index("zh"), lax.axis_index(REP)
    column = lax.axis_index(("x", "y"))
    place = jnp.stack([part, plane, column, lax.axis_index("x")]).astype(jnp.int32)
    shape = jax.ShapeDtypeStruct
    slots = 2 * pos_partner.shape[1]
    count = xy * W32

    sent = call(
        products_kernel,
        [SMEM, SMEM, VMEM, VMEM],
        shape((q * xy, W32, B), BF),
        [pltpu.VMEM((q * xy, W32, B), F32)],
    )(tile_rows, tile_live, features.T, tiles)
    recv = lax.all_to_all(sent, ROWS, 0, 0, tiled=True)

    column_part = call(
        aggregate_kernel, [SMEM, VMEM, VMEM, VMEM], shape((q * q, W32 + slots, B), BF)
    )(place, recv, pos_partner.T, neg_partner.T)
    blocks = lax.all_to_all(column_part, ("zh",) + REP, 0, 0, tiled=True)

    enodes, agg, emb_t, slab_part = call(
        functools.partial(embed_kernel, q),
        [SMEM, VMEM, VMEM],
        (
            shape((q * B, F), BF),
            shape((q, F, B), BF),
            shape((W32, B), BF),
            shape((xy, 2 * W32, B), BF),
        ),
        [pltpu.VMEM((q, F, B), BF), pltpu.VMEM((B, B), BF)],
    )(place, blocks, weight)
    slab = lax.all_to_all(slab_part, ("x", "y"), 0, 0, tiled=True)

    cpos, ctot = call(
        functools.partial(direct_kernel, q, xy),
        [SMEM, VMEM],
        (shape((q, count, B), BF), shape((q, count, B), BF)),
        flops=100000000,
    )(place, blocks)

    pieces = call(
        functools.partial(decoder_kernel, q, xy),
        [SMEM] + [VMEM] * 6,
        shape((q * q, W32 + 2 * W32 // q, B), BF),
        [
            pltpu.VMEM((count, F), BF),
            pltpu.VMEM((count, B), F32),
            pltpu.VMEM((slots, B, B), F32),
            pltpu.VMEM((count, q * B), F32),
            pltpu.VMEM((count, q * B), BF),
            pltpu.VMEM((count, q * B), BF),
        ],
    )(place, slab, enodes, agg, weight, cpos, ctot)
    mine = lax.all_to_all(pieces, ("zh",) + REP, 0, 0, tiled=True)

    height = pieces.shape[1]
    plane_part = call(functools.partial(owner_kernel, q), [VMEM], shape((q * ny, height, B), BF))(mine)
    lines = lax.all_to_all(plane_part, ("zh", "y"), 0, 0, tiled=True)

    line = call(
        functools.partial(merge_kernel, q), [VMEM], shape(((q * ny + 2) * W32, B), BF)
    )(lines)
    ahead = [line]
    for d in range(1, nx):
        ahead.append(lax.ppermute(line, "x", [(i, (i + d) % nx) for i in range(nx)]))

    gf_t, grad_weight = call(
        functools.partial(features_kernel, q, nx, ny),
        [SMEM, SMEM, SMEM] + [VMEM] * (nx + 1),
        (shape((W32, B), BF), shape((W32, F), F32)),
    )(place, tile_rows, tile_live, *ahead, tiles)
    return (emb_t.T, grad_weight, gf_t.T)


def sharded(mesh):
    return jax.shard_map(
        on_device,
        mesh=mesh,
        in_specs=(
            P(ROWS, REP),
            P(),
            P(ROWS, None, None, None),
            P(ROWS, None),
            P(ROWS, None),
            P(ROWS, None),
            P(ROWS, None),
        ),
        out_specs=(P(ROWS, REP), P(REP, None), P(ROWS, REP)),
        check_vma=False,
    )


def solution(mesh):
    rows = mesh.shape["rows"]
    parts = mesh.devices.reshape(4, 4, rows // 16, 2, 2)
    return sharded(Mesh(parts, ("zh", "x", "y", "zl", "core")))
```

```python
import functools
import math

import jax
import jax.numpy as jnp
from jax import lax
from jax.experimental import pallas as pl
from jax.experimental.pallas import tpu as pltpu
from jax.sharding import Mesh, PartitionSpec as P

BF = jnp.bfloat16
F32 = jnp.float32
B = 128
F = 128
W32 = 32
ROWS = ("zh", "x", "y")
REP = ("zl", "core")
PARAMS = pltpu.CompilerParams(vmem_limit_bytes=40 * 1024 * 1024)
VMEM = pl.BlockSpec(memory_space=pltpu.VMEM)
SMEM = pl.BlockSpec(memory_space=pltpu.SMEM)


def tn(a, b):
    return lax.dot_general(a, b, (((0,), (0,)), ((), ())), preferred_element_type=F32)


def nt(a, b):
    return lax.dot_general(a, b, (((1,), (1,)), ((), ())), preferred_element_type=F32)


def nn(a, b):
    return lax.dot_general(a, b, (((1,), (0,)), ((), ())), preferred_element_type=F32)


def call(body, in_specs, out_shape, scratch=(), flops=1000000, nbytes=1000000):
    multi = isinstance(out_shape, (tuple, list))
    return pl.pallas_call(
        body,
        out_shape=out_shape,
        in_specs=in_specs,
        out_specs=[VMEM] * len(out_shape) if multi else VMEM,
        scratch_shapes=list(scratch),
        compiler_params=PARAMS,
        cost_estimate=pl.CostEstimate(flops=flops, bytes_accessed=nbytes, transcendentals=0),
    )


def split(value):
    high = value.astype(BF).astype(F32)
    return high, value - high


def products_kernel(rows_ref, live_ref, feat_ref, tiles_ref, out_ref, acc):
    acc[...] = jnp.zeros_like(acc)
    for s in range(tiles_ref.shape[1]):
        prod = nt(feat_ref[...], tiles_ref[0, s]) * live_ref[0, s].astype(F32)
        acc[rows_ref[0, s]] += prod
    out_ref[...] = acc[...].astype(BF)


def aggregate_kernel(recv_ref, out_ref):
    total = recv_ref[0].astype(F32)
    for r in range(1, recv_ref.shape[0]):
        total = total + recv_ref[r].astype(F32)
    out_ref[...] = total.astype(BF)


def embed_kernel(place_ref, agg_ref, w_ref, pos_ref, neg_ref, embt_ref, send_ref, et_s, e_s):
    part, column = place_ref[0], place_ref[2]
    et = tn(w_ref[...], agg_ref[...])
    et_s[...] = et.astype(BF)
    e_s[...] = et.T.astype(BF)
    mine = pl.ds(pl.multiple_of(part * W32, W32), W32)
    embt_ref[...] = et_s[mine, :]
    nodes = e_s[mine, :]
    ids = jnp.concatenate([pos_ref[...], neg_ref[...]], axis=0)
    block = lax.shift_right_logical(ids, 7)
    table = jnp.concatenate([block, ids - block * B], axis=0).astype(F32)
    lane = lax.broadcasted_iota(jnp.int32, table.shape, 1)
    first = part * W32
    table = jnp.where((lane >= first) & (lane < first + W32), table, 0.0)
    quarters = B // W32
    turn = lax.rem(lax.rem(column, quarters) - part + quarters, quarters) * W32
    partners = pltpu.roll(table, turn, 1).astype(BF)
    for d in range(send_ref.shape[0]):
        send_ref[d, 0:W32, :] = nodes
        send_ref[d, W32:, :] = partners


def nodes_kernel(w_ref, *refs):
    aggs, out_ref = refs[:-1], refs[-1]
    for d, agg_ref in enumerate(aggs):
        out_ref[d * B : (d + 1) * B, :] = tn(w_ref[...], agg_ref[...]).T.astype(BF)


def direct_kernel(xy, place_ref, *refs):
    tables, (cpos_ref, ctot_ref, want_s, wide_s) = refs[:-4], refs[-4:]
    part, plane = place_ref[0], place_ref[1]
    slots = tables[0].shape[0]
    pk = slots // 2
    lane = lax.broadcasted_iota(jnp.int32, (B, B), 1).astype(F32)
    for d, table_ref in enumerate(tables):
        ids = table_ref[...]
        block = lax.shift_right_logical(ids, 7)
        piece = block - plane * xy
        place = ids - block * B - part * W32
        inside = (piece >= 0) & (piece < xy) & (place >= 0) & (place < W32)
        want = jnp.where(inside, piece * W32 + place, -1).astype(F32)
        want_s[...] = jnp.concatenate([want, jnp.zeros((B - slots, B), F32)], axis=0).T
        for k in range(slots):
            wide_s[k] = jnp.broadcast_to(want_s[:, k : k + 1], (B, B))

        def step(g, carry):
            at = lane + (g * B).astype(F32)
            cpos = jnp.zeros((B, B), F32)
            cneg = jnp.zeros((B, B), F32)
            for k in range(pk):
                cpos = jnp.where(wide_s[k] == at, cpos + 1.0, cpos)
                cneg = jnp.where(wide_s[pk + k] == at, cneg + 1.0, cneg)
            cpos_ref[g, d * B : (d + 1) * B, :] = cpos.astype(BF)
            ctot_ref[g, d * B : (d + 1) * B, :] = (cpos + cneg).astype(BF)
            return carry

        lax.fori_loop(0, cpos_ref.shape[0], step, 0)


def decoder_kernel(q, xy, slots, place_ref, got_ref, en_ref, w_ref, cpos_ref, ctot_ref, *refs):
    aggs, (out_ref, logit_s, high_s, low_s) = refs[:q], refs[q:]
    pk = slots // 2
    plane, column = place_ref[1], place_ref[2]
    quarters = B // W32
    groups = got_ref.shape[0] // quarters
    tile = 16
    sub = [
        (lax.broadcasted_iota(jnp.int32, (tile, B), 0) + i * tile).astype(F32).astype(BF)
        for i in range(B // tile)
    ]
    en = en_ref[...]
    for g in range(groups):
        em = got_ref[g * quarters : (g + 1) * quarters, 0:W32, :].reshape(B, F)
        logit_s[g] = nt(en, em)
    half = 0.5 / math.sqrt(F)
    one, zero = jnp.ones((tile, B), BF), jnp.zeros((tile, B), BF)

    def step(g, carry):
        table = got_ref[g * quarters, W32:, :].astype(F32)
        for j in range(1, quarters):
            table = table + got_ref[g * quarters + j, W32:, :].astype(F32)
        for d in range(q):
            block = lax.rem(plane - d + q, q) * xy + column
            code = jnp.where(table[:slots] == block.astype(F32), table[slots:], -1.0)
            wide = [
                jnp.broadcast_to(code[k : k + 1], (tile, B)).astype(BF) for k in range(slots)
            ]
            both, ineg = [], []
            for i in range(B // tile):
                cp, cn = zero, zero
                for k in range(pk):
                    cp = jnp.where(wide[k] == sub[i], cp + one, cp)
                    cn = jnp.where(wide[pk + k] == sub[i], cn + one, cn)
                both.append(cp)
                ineg.append(cp + cn)
            rows = slice(d * B, (d + 1) * B)
            cpos = (cpos_ref[g, rows, :] + jnp.concatenate(both, axis=0)).astype(F32)
            ctot = (ctot_ref[g, rows, :] + jnp.concatenate(ineg, axis=0)).astype(F32)
            sig = 0.5 * jnp.tanh(logit_s[g, rows, :] * half) + 0.5
            high, low = split(ctot * sig - cpos)
            high_s[g, rows, :] = high.astype(BF)
            low_s[g, rows, :] = low.astype(BF)
        return carry

    lax.fori_loop(0, groups, step, 0)
    grad = jnp.zeros((q * B, F), F32)
    for g in range(groups):
        em = got_ref[g * quarters : (g + 1) * quarters, 0:W32, :].reshape(B, F)
        grad = grad + nn(high_s[g], em) + nn(low_s[g], em)
    high, low = split(grad * (1.0 / pk))
    high, low = high.astype(BF), low.astype(BF)
    grad_agg = nt(w_ref[...], high) + nt(w_ref[...], low)
    terms = jnp.zeros((F, F), F32)
    for d in range(q):
        rows = slice(d * B, (d + 1) * B)
        terms = terms + nn(aggs[d][...], high[rows]) + nn(aggs[d][...], low[rows])
    thigh, tlow = split(terms)
    eighth = W32 // q
    for d in range(q):
        z = lax.rem(plane - d + q, q)
        for p in range(q):
            cols = grad_agg[p * W32 : (p + 1) * W32, d * B : (d + 1) * B]
            out_ref[z * q + p, 0:W32, :] = cols.astype(BF)
    for z in range(q):
        for p in range(q):
            first = p * W32 + z * eighth
            piece = [thigh[first : first + eighth], tlow[first : first + eighth]]
            out_ref[z * q + p, W32:, :] = jnp.concatenate(piece, axis=0).astype(BF)


def owner_kernel(q, got_ref, out_ref):
    total = got_ref[0].astype(F32)
    for r in range(1, got_ref.shape[0]):
        total = total + got_ref[r].astype(F32)
    eighth = W32 // q
    high, low = split(total[W32 : W32 + eighth] + total[W32 + eighth :])
    sent = jnp.concatenate([total[:W32], high, low], axis=0).astype(BF)
    for d in range(out_ref.shape[0]):
        out_ref[d] = sent


def merge_kernel(q, got_ref, out_ref):
    count = got_ref.shape[0]
    ny = count // q
    eighth = W32 // q
    blocks = got_ref[:, 0:W32, :].reshape(count * W32, B)
    rows = []
    for z in range(q):
        total = got_ref[z * ny, W32:, :].astype(F32)
        for y in range(1, ny):
            total = total + got_ref[z * ny + y, W32:, :].astype(F32)
        rows.append(total[:eighth] + total[eighth:])
    high, low = split(jnp.concatenate(rows, axis=0))
    for d in range(out_ref.shape[0]):
        out_ref[d, 0 : count * W32, :] = blocks
        out_ref[d, count * W32 : (count + 1) * W32, :] = high.astype(BF)
        out_ref[d, (count + 1) * W32 :, :] = low.astype(BF)


def features_kernel(q, nx, ny, rows_ref, live_ref, got_ref, tiles_ref, gft_ref, gw_ref):
    total = jnp.zeros((W32, B), F32)
    for s in range(tiles_ref.shape[1]):
        row = rows_ref[0, s]
        plane = lax.div(row, nx * ny)
        line = lax.rem(lax.div(row, ny), nx)
        first = pl.multiple_of((plane * ny + lax.rem(row, ny)) * W32, W32)
        live = live_ref[0, s].astype(F32)
        block = got_ref[line, pl.ds(first, W32), :].astype(F32) * live
        total = total + nn(block.astype(BF), tiles_ref[0, s])
    gft_ref[...] = total.astype(BF)
    first = q * ny * W32
    terms = got_ref[:, first : first + W32, :].astype(F32) + got_ref[:, first + W32 :, :].astype(F32)
    gw_ref[...] = jnp.sum(terms, axis=0) * (1.0 / math.sqrt(q * nx * ny * B))


def ring(value, axis, size):
    out = [value]
    for d in range(1, size):
        out.append(lax.ppermute(value, axis, [(i, (i + d) % size) for i in range(size)]))
    return out


def on_device(features, weight, tiles, tile_rows, tile_live, pos_partner, neg_partner):
    q = lax.axis_size("zh")
    nx, ny = lax.axis_size("x"), lax.axis_size("y")
    xy = nx * ny
    place = jnp.stack([lax.axis_index(REP), lax.axis_index("zh"), lax.axis_index(("x", "y"))])
    place = place.astype(jnp.int32)
    shape = jax.ShapeDtypeStruct
    slots = 2 * pos_partner.shape[1]
    groups = xy * W32 // B
    pos_t, neg_t = pos_partner.T, neg_partner.T

    sent = call(
        products_kernel,
        [SMEM, SMEM, VMEM, VMEM],
        shape((q * xy, W32, B), BF),
        [pltpu.VMEM((q * xy, W32, B), F32)],
    )(tile_rows, tile_live, features.T, tiles)
    recv = lax.all_to_all(sent, ROWS, 0, 0, tiled=True)

    tables = ring(jnp.concatenate([pos_t, neg_t], axis=0), "zh", q)
    cpos, ctot = call(
        functools.partial(direct_kernel, xy),
        [SMEM] + [VMEM] * q,
        (shape((groups, q * B, B), BF), shape((groups, q * B, B), BF)),
        [pltpu.VMEM((B, B), F32), pltpu.VMEM((slots, B, B), F32)],
        flops=100000000,
    )(place, *tables)

    agg_own = call(aggregate_kernel, [VMEM], shape((W32, B), BF))(recv)
    agg = lax.all_gather(agg_own, REP, axis=0, tiled=True)
    aggs = ring(agg, "zh", q)
    emb_t, slab_part = call(
        embed_kernel,
        [SMEM] + [VMEM] * 4,
        (shape((W32, B), BF), shape((xy, W32 + 2 * slots, B), BF)),
        [pltpu.VMEM((F, B), BF), pltpu.VMEM((B, F), BF)],
    )(place, agg, weight, pos_t, neg_t)
    slab = lax.all_to_all(slab_part, ("x", "y"), 0, 0, tiled=True)
    nodes = call(nodes_kernel, [VMEM] * (1 + q), shape((q * B, F), BF))(weight, *aggs)

    pieces = call(
        functools.partial(decoder_kernel, q, xy, slots),
        [SMEM] + [VMEM] * (5 + q),
        shape((q * q, W32 + 2 * W32 // q, B), BF),
        [
            pltpu.VMEM((groups, q * B, B), F32),
            pltpu.VMEM((groups, q * B, B), BF),
            pltpu.VMEM((groups, q * B, B), BF),
        ],
    )(place, slab, nodes, weight, cpos, ctot, *aggs)
    mine = lax.all_to_all(pieces, ("zh",) + REP, 0, 0, tiled=True)

    height = pieces.shape[1]
    plane_part = call(functools.partial(owner_kernel, q), [VMEM], shape((q * ny, height, B), BF))(mine)
    lines = lax.all_to_all(plane_part, ("zh", "y"), 0, 0, tiled=True)

    line_part = call(
        functools.partial(merge_kernel, q), [VMEM], shape((nx, (q * ny + 2) * W32, B), BF)
    )(lines)
    every = lax.all_to_all(line_part, "x", 0, 0, tiled=True)

    gf_t, grad_weight = call(
        functools.partial(features_kernel, q, nx, ny),
        [SMEM, SMEM, VMEM, VMEM],
        (shape((W32, B), BF), shape((W32, F), F32)),
    )(tile_rows, tile_live, every, tiles)
    return (emb_t.T, grad_weight, gf_t.T)


def sharded(mesh):
    return jax.shard_map(
        on_device,
        mesh=mesh,
        in_specs=(
            P(ROWS, REP),
            P(),
            P(ROWS, None, None, None),
            P(ROWS, None),
            P(ROWS, None),
            P(ROWS, None),
            P(ROWS, None),
        ),
        out_specs=(P(ROWS, REP), P(REP, None), P(ROWS, REP)),
        check_vma=False,
    )


def solution(mesh):
    rows = mesh.shape["rows"]
    parts = mesh.devices.reshape(4, 4, rows // 16, 2, 2)
    return sharded(Mesh(parts, ("zh", "x", "y", "zl", "core")))
```

```python
import functools
import math

import jax
import jax.numpy as jnp
from jax import lax
from jax.experimental import pallas as pl
from jax.experimental.pallas import tpu as pltpu
from jax.sharding import Mesh, PartitionSpec as P

BF = jnp.bfloat16
F32 = jnp.float32
B = 128
F = 128
W32 = 32
ROWS = ("zh", "x", "y")
REP = ("zl", "core")
PARAMS = pltpu.CompilerParams(vmem_limit_bytes=40 * 1024 * 1024)
VMEM = pl.BlockSpec(memory_space=pltpu.VMEM)
SMEM = pl.BlockSpec(memory_space=pltpu.SMEM)
ANY = pl.BlockSpec(memory_space=pl.ANY)


def tn(a, b):
    return lax.dot_general(a, b, (((0,), (0,)), ((), ())), preferred_element_type=F32)


def nt(a, b):
    return lax.dot_general(a, b, (((1,), (1,)), ((), ())), preferred_element_type=F32)


def nn(a, b):
    return lax.dot_general(a, b, (((1,), (0,)), ((), ())), preferred_element_type=F32)


def call(body, in_specs, out_shape, scratch=(), flops=1000000, nbytes=1000000):
    multi = isinstance(out_shape, (tuple, list))
    return pl.pallas_call(
        body,
        out_shape=out_shape,
        in_specs=in_specs,
        out_specs=[VMEM] * len(out_shape) if multi else VMEM,
        scratch_shapes=list(scratch),
        compiler_params=PARAMS,
        cost_estimate=pl.CostEstimate(flops=flops, bytes_accessed=nbytes, transcendentals=0),
    )


def split(value):
    high = value.astype(BF).astype(F32)
    return high, value - high


def products_kernel(rows_ref, live_ref, feat_ref, tiles_ref, out_ref, acc):
    acc[...] = jnp.zeros_like(acc)
    for s in range(tiles_ref.shape[1]):
        prod = nt(feat_ref[...], tiles_ref[0, s]) * live_ref[0, s].astype(F32)
        acc[rows_ref[0, s]] += prod
    out_ref[...] = acc[...].astype(BF)


def table_kernel(after_ref, pos_ref, neg_ref, out_ref):
    out_ref[...] = jnp.concatenate([pos_ref[...], neg_ref[...]], axis=0)


def aggregate_kernel(after_ref, recv_ref, out_ref):
    total = recv_ref[0].astype(F32)
    for r in range(1, recv_ref.shape[0]):
        total = total + recv_ref[r].astype(F32)
    out_ref[...] = total.astype(BF)


def embed_kernel(place_ref, agg_ref, w_ref, pos_ref, neg_ref, embt_ref, send_ref, et_s, e_s):
    part, column = place_ref[0], place_ref[2]
    et = tn(w_ref[...], agg_ref[...])
    et_s[...] = et.astype(BF)
    e_s[...] = et.T.astype(BF)
    mine = pl.ds(pl.multiple_of(part * W32, W32), W32)
    embt_ref[...] = et_s[mine, :]
    nodes = e_s[mine, :]
    ids = jnp.concatenate([pos_ref[...], neg_ref[...]], axis=0)
    block = lax.shift_right_logical(ids, 7)
    table = jnp.concatenate([block, ids - block * B], axis=0).astype(F32)
    lane = lax.broadcasted_iota(jnp.int32, table.shape, 1)
    first = part * W32
    table = jnp.where((lane >= first) & (lane < first + W32), table, 0.0)
    quarters = B // W32
    turn = lax.rem(lax.rem(column, quarters) - part + quarters, quarters) * W32
    partners = pltpu.roll(table, turn, 1).astype(BF)
    for d in range(send_ref.shape[0]):
        send_ref[d, 0:W32, :] = nodes
        send_ref[d, W32:, :] = partners


def nodes_kernel(w_ref, *refs):
    aggs, out_ref = refs[:-1], refs[-1]
    for d, agg_ref in enumerate(aggs):
        out_ref[d * B : (d + 1) * B, :] = tn(w_ref[...], agg_ref[...]).T.astype(BF)


def direct_kernel(xy, place_ref, *refs):
    tables, (cpos_ref, ctot_ref, want_s, wide_s) = refs[:-4], refs[-4:]
    part, plane = place_ref[0], place_ref[1]
    slots = tables[0].shape[0]
    pk = slots // 2
    lane = lax.broadcasted_iota(jnp.int32, (B, B), 1).astype(F32)
    for d, table_ref in enumerate(tables):
        ids = table_ref[...]
        block = lax.shift_right_logical(ids, 7)
        piece = block - plane * xy
        place = ids - block * B - part * W32
        inside = (piece >= 0) & (piece < xy) & (place >= 0) & (place < W32)
        want = jnp.where(inside, piece * W32 + place, -1).astype(F32)
        want_s[...] = jnp.concatenate([want, jnp.zeros((B - slots, B), F32)], axis=0).T
        for k in range(slots):
            wide_s[k] = jnp.broadcast_to(want_s[:, k : k + 1], (B, B))

        def step(g, carry):
            at = lane + (g * B).astype(F32)
            cpos = jnp.zeros((B, B), F32)
            cneg = jnp.zeros((B, B), F32)
            for k in range(pk):
                cpos = jnp.where(wide_s[k] == at, cpos + 1.0, cpos)
                cneg = jnp.where(wide_s[pk + k] == at, cneg + 1.0, cneg)
            cpos_ref[g, d * B : (d + 1) * B, :] = cpos.astype(BF)
            ctot_ref[g, d * B : (d + 1) * B, :] = (cpos + cneg).astype(BF)
            return carry

        lax.fori_loop(0, cpos_ref.shape[0], step, 0)


def decoder_kernel(q, xy, slots, place_ref, got_ref, en_ref, w_ref, cpos_ref, ctot_ref, *refs):
    aggs, (out_ref, logit_s, high_s, low_s) = refs[:q], refs[q:]
    pk = slots // 2
    plane, column = place_ref[1], place_ref[2]
    quarters = B // W32
    groups = got_ref.shape[0] // quarters
    tile = 16
    sub = [
        (lax.broadcasted_iota(jnp.int32, (tile, B), 0) + i * tile).astype(F32).astype(BF)
        for i in range(B // tile)
    ]
    en = en_ref[...]
    for g in range(groups):
        em = got_ref[g * quarters : (g + 1) * quarters, 0:W32, :].reshape(B, F)
        logit_s[g] = nt(en, em)
    half = 0.5 / math.sqrt(F)
    one, zero = jnp.ones((tile, B), BF), jnp.zeros((tile, B), BF)

    def step(g, carry):
        table = got_ref[g * quarters, W32:, :].astype(F32)
        for j in range(1, quarters):
            table = table + got_ref[g * quarters + j, W32:, :].astype(F32)
        for d in range(q):
            block = lax.rem(plane - d + q, q) * xy + column
            code = jnp.where(table[:slots] == block.astype(F32), table[slots:], -1.0)
            wide = [
                jnp.broadcast_to(code[k : k + 1], (tile, B)).astype(BF) for k in range(slots)
            ]
            both, ineg = [], []
            for i in range(B // tile):
                cp, cn = zero, zero
                for k in range(pk):
                    cp = jnp.where(wide[k] == sub[i], cp + one, cp)
                    cn = jnp.where(wide[pk + k] == sub[i], cn + one, cn)
                both.append(cp)
                ineg.append(cp + cn)
            rows = slice(d * B, (d + 1) * B)
            cpos = (cpos_ref[g, rows, :] + jnp.concatenate(both, axis=0)).astype(F32)
            ctot = (ctot_ref[g, rows, :] + jnp.concatenate(ineg, axis=0)).astype(F32)
            sig = 0.5 * jnp.tanh(logit_s[g, rows, :] * half) + 0.5
            high, low = split(ctot * sig - cpos)
            high_s[g, rows, :] = high.astype(BF)
            low_s[g, rows, :] = low.astype(BF)
        return carry

    lax.fori_loop(0, groups, step, 0)
    grad = jnp.zeros((q * B, F), F32)
    for g in range(groups):
        em = got_ref[g * quarters : (g + 1) * quarters, 0:W32, :].reshape(B, F)
        grad = grad + nn(high_s[g], em) + nn(low_s[g], em)
    high, low = split(grad * (1.0 / pk))
    high, low = high.astype(BF), low.astype(BF)
    grad_agg = nt(w_ref[...], high) + nt(w_ref[...], low)
    terms = jnp.zeros((F, F), F32)
    for d in range(q):
        rows = slice(d * B, (d + 1) * B)
        terms = terms + nn(aggs[d][...], high[rows]) + nn(aggs[d][...], low[rows])
    thigh, tlow = split(terms)
    eighth = W32 // q
    for d in range(q):
        z = lax.rem(plane - d + q, q)
        for p in range(q):
            cols = grad_agg[p * W32 : (p + 1) * W32, d * B : (d + 1) * B]
            out_ref[z * q + p, 0:W32, :] = cols.astype(BF)
    for z in range(q):
        for p in range(q):
            first = p * W32 + z * eighth
            piece = [thigh[first : first + eighth], tlow[first : first + eighth]]
            out_ref[z * q + p, W32:, :] = jnp.concatenate(piece, axis=0).astype(BF)


def owner_kernel(q, got_ref, out_ref):
    total = got_ref[0].astype(F32)
    for r in range(1, got_ref.shape[0]):
        total = total + got_ref[r].astype(F32)
    eighth = W32 // q
    high, low = split(total[W32 : W32 + eighth] + total[W32 + eighth :])
    sent = jnp.concatenate([total[:W32], high, low], axis=0).astype(BF)
    for d in range(out_ref.shape[0]):
        out_ref[d] = sent


def merge_kernel(q, got_ref, out_ref):
    count = got_ref.shape[0]
    ny = count // q
    eighth = W32 // q
    blocks = got_ref[:, 0:W32, :].reshape(count * W32, B)
    rows = []
    for z in range(q):
        total = got_ref[z * ny, W32:, :].astype(F32)
        for y in range(1, ny):
            total = total + got_ref[z * ny + y, W32:, :].astype(F32)
        rows.append(total[:eighth] + total[eighth:])
    high, low = split(jnp.concatenate(rows, axis=0))
    for d in range(out_ref.shape[0]):
        out_ref[d, 0 : count * W32, :] = blocks
        out_ref[d, count * W32 : (count + 1) * W32, :] = high.astype(BF)
        out_ref[d, (count + 1) * W32 :, :] = low.astype(BF)


def features_kernel(q, nx, ny, rows_ref, live_ref, got_ref, tiles_ref, gft_ref, gw_ref):
    total = jnp.zeros((W32, B), F32)
    for s in range(tiles_ref.shape[1]):
        row = rows_ref[0, s]
        plane = lax.div(row, nx * ny)
        line = lax.rem(lax.div(row, ny), nx)
        first = pl.multiple_of((plane * ny + lax.rem(row, ny)) * W32, W32)
        live = live_ref[0, s].astype(F32)
        block = got_ref[line, pl.ds(first, W32), :].astype(F32) * live
        total = total + nn(block.astype(BF), tiles_ref[0, s])
    gft_ref[...] = total.astype(BF)
    first = q * ny * W32
    terms = got_ref[:, first : first + W32, :].astype(F32) + got_ref[:, first + W32 :, :].astype(F32)
    gw_ref[...] = jnp.sum(terms, axis=0) * (1.0 / math.sqrt(q * nx * ny * B))


def ring(value, axis, size):
    out = [value]
    for d in range(1, size):
        out.append(lax.ppermute(value, axis, [(i, (i + d) % size) for i in range(size)]))
    return out


def on_device(features, weight, tiles, tile_rows, tile_live, pos_partner, neg_partner):
    q = lax.axis_size("zh")
    nx, ny = lax.axis_size("x"), lax.axis_size("y")
    xy = nx * ny
    place = jnp.stack([lax.axis_index(REP), lax.axis_index("zh"), lax.axis_index(("x", "y"))])
    place = place.astype(jnp.int32)
    shape = jax.ShapeDtypeStruct
    slots = 2 * pos_partner.shape[1]
    groups = xy * W32 // B
    pos_t, neg_t = pos_partner.T, neg_partner.T

    sent = call(
        products_kernel,
        [SMEM, SMEM, VMEM, VMEM],
        shape((q * xy, W32, B), BF),
        [pltpu.VMEM((q * xy, W32, B), F32)],
    )(tile_rows, tile_live, features.T, tiles)
    recv = lax.all_to_all(sent, ROWS, 0, 0, tiled=True)

    table = call(table_kernel, [ANY, VMEM, VMEM], shape((slots, B), jnp.int32))(sent, pos_t, neg_t)
    tables = ring(table, "zh", q)
    cpos, ctot = call(
        functools.partial(direct_kernel, xy),
        [SMEM] + [VMEM] * q,
        (shape((groups, q * B, B), BF), shape((groups, q * B, B), BF)),
        [pltpu.VMEM((B, B), F32), pltpu.VMEM((slots, B, B), F32)],
        flops=100000000,
    )(place, *tables)

    agg_own = call(aggregate_kernel, [ANY, VMEM], shape((W32, B), BF))(cpos, recv)
    agg = lax.all_gather(agg_own, REP, axis=0, tiled=True)
    aggs = ring(agg, "zh", q)
    emb_t, slab_part = call(
        embed_kernel,
        [SMEM] + [VMEM] * 4,
        (shape((W32, B), BF), shape((xy, W32 + 2 * slots, B), BF)),
        [pltpu.VMEM((F, B), BF), pltpu.VMEM((B, F), BF)],
    )(place, agg, weight, pos_t, neg_t)
    slab = lax.all_to_all(slab_part, ("x", "y"), 0, 0, tiled=True)
    nodes = call(nodes_kernel, [VMEM] * (1 + q), shape((q * B, F), BF))(weight, *aggs)

    pieces = call(
        functools.partial(decoder_kernel, q, xy, slots),
        [SMEM] + [VMEM] * (5 + q),
        shape((q * q, W32 + 2 * W32 // q, B), BF),
        [
            pltpu.VMEM((groups, q * B, B), F32),
            pltpu.VMEM((groups, q * B, B), BF),
            pltpu.VMEM((groups, q * B, B), BF),
        ],
    )(place, slab, nodes, weight, cpos, ctot, *aggs)
    mine = lax.all_to_all(pieces, ("zh",) + REP, 0, 0, tiled=True)

    height = pieces.shape[1]
    plane_part = call(functools.partial(owner_kernel, q), [VMEM], shape((q * ny, height, B), BF))(mine)
    lines = lax.all_to_all(plane_part, ("zh", "y"), 0, 0, tiled=True)

    line_part = call(
        functools.partial(merge_kernel, q), [VMEM], shape((nx, (q * ny + 2) * W32, B), BF)
    )(lines)
    every = lax.all_to_all(line_part, "x", 0, 0, tiled=True)

    gf_t, grad_weight = call(
        functools.partial(features_kernel, q, nx, ny),
        [SMEM, SMEM, VMEM, VMEM],
        (shape((W32, B), BF), shape((W32, F), F32)),
    )(tile_rows, tile_live, every, tiles)
    return (emb_t.T, grad_weight, gf_t.T)


def sharded(mesh):
    return jax.shard_map(
        on_device,
        mesh=mesh,
        in_specs=(
            P(ROWS, REP),
            P(),
            P(ROWS, None, None, None),
            P(ROWS, None),
            P(ROWS, None),
            P(ROWS, None),
            P(ROWS, None),
        ),
        out_specs=(P(ROWS, REP), P(REP, None), P(ROWS, REP)),
        check_vma=False,
    )


def solution(mesh):
    rows = mesh.shape["rows"]
    parts = mesh.devices.reshape(4, 4, rows // 16, 2, 2)
    return sharded(Mesh(parts, ("zh", "x", "y", "zl", "core")))
```

```python
import functools
import math

import jax
import jax.numpy as jnp
from jax import lax
from jax.experimental import pallas as pl
from jax.experimental.pallas import tpu as pltpu
from jax.sharding import Mesh, PartitionSpec as P

BF = jnp.bfloat16
F32 = jnp.float32
B = 128
F = 128
W32 = 32
NEAR = ("x", "yl")
FAR = ("zh", "yh")
COLUMN = ("x", "yh", "yl")
ROWS = ("zh",) + COLUMN
REP = ("zl", "core")
PARAMS = pltpu.CompilerParams(vmem_limit_bytes=40 * 1024 * 1024)
VMEM = pl.BlockSpec(memory_space=pltpu.VMEM)
SMEM = pl.BlockSpec(memory_space=pltpu.SMEM)
ANY = pl.BlockSpec(memory_space=pl.ANY)


def tn(a, b):
    return lax.dot_general(a, b, (((0,), (0,)), ((), ())), preferred_element_type=F32)


def nt(a, b):
    return lax.dot_general(a, b, (((1,), (1,)), ((), ())), preferred_element_type=F32)


def nn(a, b):
    return lax.dot_general(a, b, (((1,), (0,)), ((), ())), preferred_element_type=F32)


def call(body, in_specs, out_shape, scratch=(), flops=1000000, nbytes=1000000):
    multi = isinstance(out_shape, (tuple, list))
    return pl.pallas_call(
        body,
        out_shape=out_shape,
        in_specs=in_specs,
        out_specs=[VMEM] * len(out_shape) if multi else VMEM,
        scratch_shapes=list(scratch),
        compiler_params=PARAMS,
        cost_estimate=pl.CostEstimate(flops=flops, bytes_accessed=nbytes, transcendentals=0),
    )


def split(value):
    high = value.astype(BF).astype(F32)
    return high, value - high


def products_kernel(nx, nh, nl, rows_ref, live_ref, feat_ref, tiles_ref, out_ref, acc):
    out_ref[...] = jnp.zeros_like(out_ref)
    slots = tiles_ref.shape[1]
    places = []
    for s in range(slots):
        row = rows_ref[0, s]
        plane, column = lax.div(row, nx * nh * nl), lax.rem(row, nx * nh * nl)
        line, place = lax.div(column, nh * nl), lax.rem(column, nh * nl)
        near = line * nl + lax.rem(place, nl)
        places.append((near, plane * nh + lax.div(place, nl)))
        acc[places[s]] = jnp.zeros((W32, B), F32)
    for s in range(slots):
        acc[places[s]] += nt(feat_ref[...], tiles_ref[0, s]) * live_ref[0, s].astype(F32)
    for s in range(slots):
        out_ref[places[s]] = acc[places[s]].astype(BF)


def near_kernel(recv_ref, out_ref):
    total = recv_ref[0].astype(F32)
    for r in range(1, recv_ref.shape[0]):
        total = total + recv_ref[r].astype(F32)
    out_ref[...] = total.astype(BF)


def table_kernel(after_ref, pos_ref, neg_ref, out_ref):
    out_ref[...] = jnp.concatenate([pos_ref[...], neg_ref[...]], axis=0)


def aggregate_kernel(after_ref, recv_ref, out_ref):
    total = recv_ref[0].astype(F32)
    for r in range(1, recv_ref.shape[0]):
        total = total + recv_ref[r].astype(F32)
    out_ref[...] = total.astype(BF)


def embed_kernel(place_ref, agg_ref, w_ref, pos_ref, neg_ref, embt_ref, send_ref, et_s, e_s):
    part, column = place_ref[0], place_ref[2]
    et = tn(w_ref[...], agg_ref[...])
    et_s[...] = et.astype(BF)
    e_s[...] = et.T.astype(BF)
    mine = pl.ds(pl.multiple_of(part * W32, W32), W32)
    embt_ref[...] = et_s[mine, :]
    nodes = e_s[mine, :]
    ids = jnp.concatenate([pos_ref[...], neg_ref[...]], axis=0)
    block = lax.shift_right_logical(ids, 7)
    table = jnp.concatenate([block, ids - block * B], axis=0).astype(F32)
    lane = lax.broadcasted_iota(jnp.int32, table.shape, 1)
    first = part * W32
    table = jnp.where((lane >= first) & (lane < first + W32), table, 0.0)
    quarters = B // W32
    turn = lax.rem(lax.rem(column, quarters) - part + quarters, quarters) * W32
    partners = pltpu.roll(table, turn, 1).astype(BF)
    for d in range(send_ref.shape[0]):
        send_ref[d, 0:W32, :] = nodes
        send_ref[d, W32:, :] = partners


def nodes_kernel(w_ref, *refs):
    aggs, out_ref = refs[:-1], refs[-1]
    for d, agg_ref in enumerate(aggs):
        out_ref[d * B : (d + 1) * B, :] = tn(w_ref[...], agg_ref[...]).T.astype(BF)


def direct_kernel(xy, place_ref, *refs):
    tables, (cpos_ref, ctot_ref, want_s, wide_s) = refs[1:-4], refs[-4:]
    part, plane = place_ref[0], place_ref[1]
    slots = tables[0].shape[0]
    pk = slots // 2
    lane = lax.broadcasted_iota(jnp.int32, (B, B), 1).astype(F32)
    for d, table_ref in enumerate(tables):
        ids = table_ref[...]
        block = lax.shift_right_logical(ids, 7)
        piece = block - plane * xy
        place = ids - block * B - part * W32
        inside = (piece >= 0) & (piece < xy) & (place >= 0) & (place < W32)
        want = jnp.where(inside, piece * W32 + place, -1).astype(F32)
        want_s[...] = jnp.concatenate([want, jnp.zeros((B - slots, B), F32)], axis=0).T
        for k in range(slots):
            wide_s[k] = jnp.broadcast_to(want_s[:, k : k + 1], (B, B))

        def step(g, carry):
            at = lane + (g * B).astype(F32)
            cpos = jnp.zeros((B, B), F32)
            cneg = jnp.zeros((B, B), F32)
            for k in range(pk):
                cpos = jnp.where(wide_s[k] == at, cpos + 1.0, cpos)
                cneg = jnp.where(wide_s[pk + k] == at, cneg + 1.0, cneg)
            cpos_ref[g, d * B : (d + 1) * B, :] = cpos.astype(BF)
            ctot_ref[g, d * B : (d + 1) * B, :] = (cpos + cneg).astype(BF)
            return carry

        lax.fori_loop(0, cpos_ref.shape[0], step, 0)


def decoder_kernel(q, xy, slots, place_ref, got_ref, en_ref, w_ref, cpos_ref, ctot_ref, *refs):
    aggs, (out_ref, logit_s, high_s, low_s) = refs[:q], refs[q:]
    pk = slots // 2
    plane, column = place_ref[1], place_ref[2]
    quarters = B // W32
    groups = got_ref.shape[0] // quarters
    tile = 16
    sub = [
        (lax.broadcasted_iota(jnp.int32, (tile, B), 0) + i * tile).astype(F32).astype(BF)
        for i in range(B // tile)
    ]
    en = en_ref[...]
    for g in range(groups):
        em = got_ref[g * quarters : (g + 1) * quarters, 0:W32, :].reshape(B, F)
        logit_s[g] = nt(en, em)
    half = 0.5 / math.sqrt(F)
    one, zero = jnp.ones((tile, B), BF), jnp.zeros((tile, B), BF)

    def step(g, carry):
        table = got_ref[g * quarters, W32:, :].astype(F32)
        for j in range(1, quarters):
            table = table + got_ref[g * quarters + j, W32:, :].astype(F32)
        for d in range(q):
            block = lax.rem(plane - d + q, q) * xy + column
            code = jnp.where(table[:slots] == block.astype(F32), table[slots:], -1.0)
            wide = [
                jnp.broadcast_to(code[k : k + 1], (tile, B)).astype(BF) for k in range(slots)
            ]
            both, ineg = [], []
            for i in range(B // tile):
                cp, cn = zero, zero
                for k in range(pk):
                    cp = jnp.where(wide[k] == sub[i], cp + one, cp)
                    cn = jnp.where(wide[pk + k] == sub[i], cn + one, cn)
                both.append(cp)
                ineg.append(cp + cn)
            rows = slice(d * B, (d + 1) * B)
            cpos = (cpos_ref[g, rows, :] + jnp.concatenate(both, axis=0)).astype(F32)
            ctot = (ctot_ref[g, rows, :] + jnp.concatenate(ineg, axis=0)).astype(F32)
            sig = 0.5 * jnp.tanh(logit_s[g, rows, :] * half) + 0.5
            high, low = split(ctot * sig - cpos)
            high_s[g, rows, :] = high.astype(BF)
            low_s[g, rows, :] = low.astype(BF)
        return carry

    lax.fori_loop(0, groups, step, 0)
    grad = jnp.zeros((q * B, F), F32)
    for g in range(groups):
        em = got_ref[g * quarters : (g + 1) * quarters, 0:W32, :].reshape(B, F)
        grad = grad + nn(high_s[g], em) + nn(low_s[g], em)
    high, low = split(grad * (1.0 / pk))
    high, low = high.astype(BF), low.astype(BF)
    grad_agg = nt(w_ref[...], high) + nt(w_ref[...], low)
    terms = jnp.zeros((F, F), F32)
    for d in range(q):
        rows = slice(d * B, (d + 1) * B)
        terms = terms + nn(aggs[d][...], high[rows]) + nn(aggs[d][...], low[rows])
    thigh, tlow = split(terms)
    eighth = W32 // q
    for d in range(q):
        z = lax.rem(plane - d + q, q)
        for p in range(q):
            cols = grad_agg[p * W32 : (p + 1) * W32, d * B : (d + 1) * B]
            out_ref[z * q + p, 0:W32, :] = cols.astype(BF)
    for z in range(q):
        for p in range(q):
            first = p * W32 + z * eighth
            piece = [thigh[first : first + eighth], tlow[first : first + eighth]]
            out_ref[z * q + p, W32:, :] = jnp.concatenate(piece, axis=0).astype(BF)


def owner_kernel(q, got_ref, out_ref):
    total = got_ref[0].astype(F32)
    for r in range(1, got_ref.shape[0]):
        total = total + got_ref[r].astype(F32)
    eighth = W32 // q
    high, low = split(total[W32 : W32 + eighth] + total[W32 + eighth :])
    sent = jnp.concatenate([total[:W32], high, low], axis=0).astype(BF)
    for d in range(out_ref.shape[0]):
        out_ref[d] = sent


def merge_kernel(q, got_ref, out_ref):
    count = got_ref.shape[0]
    nh = count // q
    eighth = W32 // q
    blocks = got_ref[:, 0:W32, :].reshape(count * W32, B)
    rows = []
    for z in range(q):
        total = got_ref[z * nh, W32:, :].astype(F32)
        for h in range(1, nh):
            total = total + got_ref[z * nh + h, W32:, :].astype(F32)
        rows.append(total[:eighth] + total[eighth:])
    high, low = split(jnp.concatenate(rows, axis=0))
    for d in range(out_ref.shape[0]):
        out_ref[d, 0 : count * W32, :] = blocks
        out_ref[d, count * W32 : (count + 1) * W32, :] = high.astype(BF)
        out_ref[d, (count + 1) * W32 :, :] = low.astype(BF)


def features_kernel(q, nx, nh, nl, rows_ref, live_ref, got_ref, tiles_ref, gft_ref, gw_ref):
    total = jnp.zeros((W32, B), F32)
    for s in range(tiles_ref.shape[1]):
        row = rows_ref[0, s]
        plane, column = lax.div(row, nx * nh * nl), lax.rem(row, nx * nh * nl)
        line, place = lax.div(column, nh * nl), lax.rem(column, nh * nl)
        near = line * nl + lax.rem(place, nl)
        first = pl.multiple_of((plane * nh + lax.div(place, nl)) * W32, W32)
        live = live_ref[0, s].astype(F32)
        block = got_ref[near, pl.ds(first, W32), :].astype(F32) * live
        total = total + nn(block.astype(BF), tiles_ref[0, s])
    gft_ref[...] = total.astype(BF)
    first = q * nh * W32
    terms = got_ref[:, first : first + W32, :].astype(F32) + got_ref[:, first + W32 :, :].astype(F32)
    gw_ref[...] = jnp.sum(terms, axis=0) * (1.0 / math.sqrt(q * nx * nh * nl * B))


def ring(value, axis, size):
    out = [value]
    for d in range(1, size):
        out.append(lax.ppermute(value, axis, [(i, (i + d) % size) for i in range(size)]))
    return out


def on_device(features, weight, tiles, tile_rows, tile_live, pos_partner, neg_partner):
    q, nx = lax.axis_size("zh"), lax.axis_size("x")
    nh, nl = lax.axis_size("yh"), lax.axis_size("yl")
    xy, near, far = nx * nh * nl, nx * nl, q * nh
    place = jnp.stack([lax.axis_index(REP), lax.axis_index("zh"), lax.axis_index(COLUMN)])
    place = place.astype(jnp.int32)
    shape = jax.ShapeDtypeStruct
    slots = 2 * pos_partner.shape[1]
    groups = xy * W32 // B
    pos_t, neg_t = pos_partner.T, neg_partner.T

    sent = call(
        functools.partial(products_kernel, nx, nh, nl),
        [SMEM, SMEM, VMEM, VMEM],
        shape((near, far, W32, B), BF),
        [pltpu.VMEM((near, far, W32, B), F32)],
    )(tile_rows, tile_live, features.T, tiles)
    near_recv = lax.all_to_all(sent.reshape(near, far * W32, B), NEAR, 0, 0, tiled=True)

    table = call(table_kernel, [ANY, VMEM, VMEM], shape((slots, B), jnp.int32))(sent, pos_t, neg_t)
    tables = ring(table, "zh", q)
    near_sum = call(near_kernel, [VMEM], shape((far * W32, B), BF))(near_recv)
    recv = lax.all_to_all(near_sum.reshape(far, W32, B), FAR, 0, 0, tiled=True)
    cpos, ctot = call(
        functools.partial(direct_kernel, xy),
        [SMEM, ANY] + [VMEM] * q,
        (shape((groups, q * B, B), BF), shape((groups, q * B, B), BF)),
        [pltpu.VMEM((B, B), F32), pltpu.VMEM((slots, B, B), F32)],
        flops=100000000,
    )(place, near_sum, *tables)

    agg_own = call(aggregate_kernel, [ANY, VMEM], shape((W32, B), BF))(cpos, recv)
    agg = lax.all_gather(agg_own, REP, axis=0, tiled=True)
    aggs = ring(agg, "zh", q)
    emb_t, slab_part = call(
        embed_kernel,
        [SMEM] + [VMEM] * 4,
        (shape((W32, B), BF), shape((xy, W32 + 2 * slots, B), BF)),
        [pltpu.VMEM((F, B), BF), pltpu.VMEM((B, F), BF)],
    )(place, agg, weight, pos_t, neg_t)
    slab = lax.all_to_all(slab_part, COLUMN, 0, 0, tiled=True)
    nodes = call(nodes_kernel, [VMEM] * (1 + q), shape((q * B, F), BF))(weight, *aggs)

    pieces = call(
        functools.partial(decoder_kernel, q, xy, slots),
        [SMEM] + [VMEM] * (5 + q),
        shape((q * q, W32 + 2 * W32 // q, B), BF),
        [
            pltpu.VMEM((groups, q * B, B), F32),
            pltpu.VMEM((groups, q * B, B), BF),
            pltpu.VMEM((groups, q * B, B), BF),
        ],
    )(place, slab, nodes, weight, cpos, ctot, *aggs)
    mine = lax.all_to_all(pieces, ("zh",) + REP, 0, 0, tiled=True)

    height = pieces.shape[1]
    far_part = call(functools.partial(owner_kernel, q), [VMEM], shape((far, height, B), BF))(mine)
    lines = lax.all_to_all(far_part, FAR, 0, 0, tiled=True)
    near_part = call(
        functools.partial(merge_kernel, q), [VMEM], shape((near, (far + 2) * W32, B), BF)
    )(lines)
    every = lax.all_to_all(near_part, NEAR, 0, 0, tiled=True)

    gf_t, grad_weight = call(
        functools.partial(features_kernel, q, nx, nh, nl),
        [SMEM, SMEM, VMEM, VMEM],
        (shape((W32, B), BF), shape((W32, F), F32)),
    )(tile_rows, tile_live, every, tiles)
    return (emb_t.T, grad_weight, gf_t.T)


def sharded(mesh):
    return jax.shard_map(
        on_device,
        mesh=mesh,
        in_specs=(
            P(ROWS, REP),
            P(),
            P(ROWS, None, None, None),
            P(ROWS, None),
            P(ROWS, None),
            P(ROWS, None),
            P(ROWS, None),
        ),
        out_specs=(P(ROWS, REP), P(REP, None), P(ROWS, REP)),
        check_vma=False,
    )


def solution(mesh):
    rows = mesh.shape["rows"]
    parts = mesh.devices.reshape(4, 4, rows // 32, 2, 2, 2)
    return sharded(Mesh(parts, ROWS + REP))
```

```python
import functools
import math

import jax
import jax.numpy as jnp
from jax import lax
from jax.experimental import pallas as pl
from jax.experimental.pallas import tpu as pltpu
from jax.sharding import Mesh, PartitionSpec as P

BF = jnp.bfloat16
F32 = jnp.float32
B = 128
F = 128
W32 = 32
NEAR = ("x", "yl")
FAR = ("zh", "yh")
COLUMN = ("x", "yh", "yl")
ROWS = ("zh",) + COLUMN
REP = ("zl", "core")
PARAMS = pltpu.CompilerParams(vmem_limit_bytes=40 * 1024 * 1024)
VMEM = pl.BlockSpec(memory_space=pltpu.VMEM)
SMEM = pl.BlockSpec(memory_space=pltpu.SMEM)


def tn(a, b):
    return lax.dot_general(a, b, (((0,), (0,)), ((), ())), preferred_element_type=F32)


def nt(a, b):
    return lax.dot_general(a, b, (((1,), (1,)), ((), ())), preferred_element_type=F32)


def nn(a, b):
    return lax.dot_general(a, b, (((1,), (0,)), ((), ())), preferred_element_type=F32)


def call(body, in_specs, out_shape, scratch=(), flops=1000000, nbytes=1000000):
    multi = isinstance(out_shape, (tuple, list))
    return pl.pallas_call(
        body,
        out_shape=out_shape,
        in_specs=in_specs,
        out_specs=[VMEM] * len(out_shape) if multi else VMEM,
        scratch_shapes=list(scratch),
        compiler_params=PARAMS,
        cost_estimate=pl.CostEstimate(flops=flops, bytes_accessed=nbytes, transcendentals=0),
    )


def split(value):
    high = value.astype(BF).astype(F32)
    return high, value - high


def products_kernel(nx, nh, nl, rows_ref, live_ref, feat_ref, tiles_ref, out_ref, acc):
    out_ref[...] = jnp.zeros_like(out_ref)
    slots = tiles_ref.shape[1]
    places = []
    for s in range(slots):
        row = rows_ref[0, s]
        plane, column = lax.div(row, nx * nh * nl), lax.rem(row, nx * nh * nl)
        line, place = lax.div(column, nh * nl), lax.rem(column, nh * nl)
        near = line * nl + lax.rem(place, nl)
        places.append((near, plane * nh + lax.div(place, nl)))
        acc[places[s]] = jnp.zeros((W32, B), F32)
    for s in range(slots):
        acc[places[s]] += nt(feat_ref[...], tiles_ref[0, s]) * live_ref[0, s].astype(F32)
    for s in range(slots):
        out_ref[places[s]] = acc[places[s]].astype(BF)


def near_kernel(q, place_ref, recv_ref, pos_ref, neg_ref, out_ref):
    far = out_ref.shape[0]
    nh = far // q
    total = recv_ref[0].astype(F32)
    for r in range(1, recv_ref.shape[0]):
        total = total + recv_ref[r].astype(F32)
    total = total.astype(BF)
    ids = jnp.concatenate([pos_ref[...], neg_ref[...]], axis=0)
    block = lax.shift_right_logical(ids, 7)
    table = jnp.where(lax.rem(place_ref[0], 2) == 0, block, ids - block * B).astype(F32).astype(BF)
    for d in range(far):
        h = d % nh
        for b in range(q):
            first = (b * nh + h) * W32
            out_ref[d, b * W32 : (b + 1) * W32, :] = total[first : first + W32]
        out_ref[d, q * W32 :, :] = table


def aggregate_kernel(q, place_ref, recv_ref, out_ref):
    far = recv_ref.shape[0]
    nh = far // q
    slots = recv_ref.shape[1] - q * W32
    total = recv_ref[0, 0 : q * W32, :].astype(F32)
    for r in range(1, far):
        total = total + recv_ref[r, 0 : q * W32, :].astype(F32)
    out_ref[0 : q * W32, :] = total.astype(BF)
    for b in range(q):
        first = q * W32 + b * slots
        out_ref[first : first + slots, :] = recv_ref[b * nh + place_ref[3], q * W32 :, :]


def embed_kernel(
    q, place_ref, got_ref, w_ref, pos_ref, neg_ref, nodes_ref, agg_ref, embt_ref, send_ref, et_s
):
    part, plane, column = place_ref[0], place_ref[1], place_ref[2]
    for b in range(q):
        for p in range(q):
            agg_ref[b, p * W32 : (p + 1) * W32, :] = got_ref[p, b * W32 : (b + 1) * W32, :]
        et = tn(w_ref[...], agg_ref[b])
        et_s[b] = et.astype(BF)
        nodes_ref[b * B : (b + 1) * B, :] = et.T.astype(BF)
    embt_ref[...] = et_s[plane, pl.ds(pl.multiple_of(part * W32, W32), W32), :]
    nodes = nodes_ref[pl.ds(pl.multiple_of(plane * B + part * W32, W32), W32), :]
    ids = jnp.concatenate([pos_ref[...], neg_ref[...]], axis=0)
    block = lax.shift_right_logical(ids, 7)
    table = jnp.concatenate([block, ids - block * B], axis=0).astype(F32)
    lane = lax.broadcasted_iota(jnp.int32, table.shape, 1)
    first = part * W32
    table = jnp.where((lane >= first) & (lane < first + W32), table, 0.0)
    quarters = B // W32
    turn = lax.rem(lax.rem(column, quarters) - part + quarters, quarters) * W32
    partners = pltpu.roll(table, turn, 1).astype(BF)
    for d in range(send_ref.shape[0]):
        send_ref[d, 0:W32, :] = nodes
        send_ref[d, W32:, :] = partners


def direct_kernel(q, xy, slots, place_ref, got_ref, cpos_ref, ctot_ref, want_s, wide_s):
    part, plane = place_ref[0], place_ref[1]
    pk = slots // 2
    lane = lax.broadcasted_iota(jnp.int32, (B, B), 1).astype(F32)
    first_block = (plane * xy).astype(F32)
    first_place = (part * W32).astype(F32)
    for d in range(q):
        rows = slice(q * W32 + d * slots, q * W32 + (d + 1) * slots)
        piece = got_ref[0, rows, :].astype(F32) - first_block
        place = got_ref[1, rows, :].astype(F32) - first_place
        inside = (piece >= 0.0) & (piece < float(xy)) & (place >= 0.0) & (place < float(W32))
        want = jnp.where(inside, piece * W32 + place, -1.0)
        want_s[...] = jnp.concatenate([want, jnp.zeros((B - slots, B), F32)], axis=0).T
        for k in range(slots):
            wide_s[k] = jnp.broadcast_to(want_s[:, k : k + 1], (B, B))

        def step(g, carry):
            at = lane + (g * B).astype(F32)
            cpos = jnp.zeros((B, B), F32)
            cneg = jnp.zeros((B, B), F32)
            for k in range(pk):
                cpos = jnp.where(wide_s[k] == at, cpos + 1.0, cpos)
                cneg = jnp.where(wide_s[pk + k] == at, cneg + 1.0, cneg)
            cpos_ref[g, d * B : (d + 1) * B, :] = cpos.astype(BF)
            ctot_ref[g, d * B : (d + 1) * B, :] = (cpos + cneg).astype(BF)
            return carry

        lax.fori_loop(0, cpos_ref.shape[0], step, 0)


def decoder_kernel(
    q, xy, slots, place_ref, got_ref, en_ref, agg_ref, w_ref, cpos_ref, ctot_ref,
    out_ref, logit_s, high_s, low_s,
):
    pk = slots // 2
    column = place_ref[2]
    quarters = B // W32
    groups = got_ref.shape[0] // quarters
    tile = 16
    sub = [
        (lax.broadcasted_iota(jnp.int32, (tile, B), 0) + i * tile).astype(F32).astype(BF)
        for i in range(B // tile)
    ]
    en = en_ref[...]
    for g in range(groups):
        em = got_ref[g * quarters : (g + 1) * quarters, 0:W32, :].reshape(B, F)
        logit_s[g] = nt(en, em)
    half = 0.5 / math.sqrt(F)
    one, zero = jnp.ones((tile, B), BF), jnp.zeros((tile, B), BF)

    def step(g, carry):
        table = got_ref[g * quarters, W32:, :].astype(F32)
        for j in range(1, quarters):
            table = table + got_ref[g * quarters + j, W32:, :].astype(F32)
        for d in range(q):
            block = d * xy + column
            code = jnp.where(table[:slots] == block.astype(F32), table[slots:], -1.0)
            wide = [
                jnp.broadcast_to(code[k : k + 1], (tile, B)).astype(BF) for k in range(slots)
            ]
            both, ineg = [], []
            for i in range(B // tile):
                cp, cn = zero, zero
                for k in range(pk):
                    cp = jnp.where(wide[k] == sub[i], cp + one, cp)
                    cn = jnp.where(wide[pk + k] == sub[i], cn + one, cn)
                both.append(cp)
                ineg.append(cp + cn)
            rows = slice(d * B, (d + 1) * B)
            cpos = (cpos_ref[g, rows, :] + jnp.concatenate(both, axis=0)).astype(F32)
            ctot = (ctot_ref[g, rows, :] + jnp.concatenate(ineg, axis=0)).astype(F32)
            sig = 0.5 * jnp.tanh(logit_s[g, rows, :] * half) + 0.5
            high, low = split(ctot * sig - cpos)
            high_s[g, rows, :] = high.astype(BF)
            low_s[g, rows, :] = low.astype(BF)
        return carry

    lax.fori_loop(0, groups, step, 0)
    grad = jnp.zeros((q * B, F), F32)
    for g in range(groups):
        em = got_ref[g * quarters : (g + 1) * quarters, 0:W32, :].reshape(B, F)
        grad = grad + nn(high_s[g], em) + nn(low_s[g], em)
    high, low = split(grad * (1.0 / pk))
    high, low = high.astype(BF), low.astype(BF)
    grad_agg = nt(w_ref[...], high) + nt(w_ref[...], low)
    terms = jnp.zeros((F, F), F32)
    for d in range(q):
        rows = slice(d * B, (d + 1) * B)
        terms = terms + nn(agg_ref[d], high[rows]) + nn(agg_ref[d], low[rows])
    thigh, tlow = split(terms)
    eighth = W32 // q
    for z in range(q):
        for p in range(q):
            cols = grad_agg[p * W32 : (p + 1) * W32, z * B : (z + 1) * B]
            out_ref[z * q + p, 0:W32, :] = cols.astype(BF)
            first = p * W32 + z * eighth
            piece = [thigh[first : first + eighth], tlow[first : first + eighth]]
            out_ref[z * q + p, W32:, :] = jnp.concatenate(piece, axis=0).astype(BF)


def owner_kernel(q, got_ref, out_ref):
    total = got_ref[0].astype(F32)
    for r in range(1, got_ref.shape[0]):
        total = total + got_ref[r].astype(F32)
    eighth = W32 // q
    high, low = split(total[W32 : W32 + eighth] + total[W32 + eighth :])
    sent = jnp.concatenate([total[:W32], high, low], axis=0).astype(BF)
    for d in range(out_ref.shape[0]):
        out_ref[d] = sent


def merge_kernel(q, got_ref, out_ref):
    count = got_ref.shape[0]
    nh = count // q
    eighth = W32 // q
    blocks = got_ref[:, 0:W32, :].reshape(count * W32, B)
    rows = []
    for z in range(q):
        total = got_ref[z * nh, W32:, :].astype(F32)
        for h in range(1, nh):
            total = total + got_ref[z * nh + h, W32:, :].astype(F32)
        rows.append(total[:eighth] + total[eighth:])
    high, low = split(jnp.concatenate(rows, axis=0))
    for d in range(out_ref.shape[0]):
        out_ref[d, 0 : count * W32, :] = blocks
        out_ref[d, count * W32 : (count + 1) * W32, :] = high.astype(BF)
        out_ref[d, (count + 1) * W32 :, :] = low.astype(BF)


def features_kernel(q, nx, nh, nl, rows_ref, live_ref, got_ref, tiles_ref, gft_ref, gw_ref):
    total = jnp.zeros((W32, B), F32)
    for s in range(tiles_ref.shape[1]):
        row = rows_ref[0, s]
        plane, column = lax.div(row, nx * nh * nl), lax.rem(row, nx * nh * nl)
        line, place = lax.div(column, nh * nl), lax.rem(column, nh * nl)
        near = line * nl + lax.rem(place, nl)
        first = pl.multiple_of((plane * nh + lax.div(place, nl)) * W32, W32)
        live = live_ref[0, s].astype(F32)
        block = got_ref[near, pl.ds(first, W32), :].astype(F32) * live
        total = total + nn(block.astype(BF), tiles_ref[0, s])
    gft_ref[...] = total.astype(BF)
    first = q * nh * W32
    terms = got_ref[:, first : first + W32, :].astype(F32) + got_ref[:, first + W32 :, :].astype(F32)
    gw_ref[...] = jnp.sum(terms, axis=0) * (1.0 / math.sqrt(q * nx * nh * nl * B))


def on_device(features, weight, tiles, tile_rows, tile_live, pos_partner, neg_partner):
    q, nx = lax.axis_size("zh"), lax.axis_size("x")
    nh, nl = lax.axis_size("yh"), lax.axis_size("yl")
    xy, near, far = nx * nh * nl, nx * nl, q * nh
    axes = (REP, "zh", COLUMN, "yh")
    place = jnp.stack([lax.axis_index(axis) for axis in axes]).astype(jnp.int32)
    shape = jax.ShapeDtypeStruct
    slots = 2 * pos_partner.shape[1]
    groups = xy * W32 // B
    pos_t, neg_t = pos_partner.T, neg_partner.T

    sent = call(
        functools.partial(products_kernel, nx, nh, nl),
        [SMEM, SMEM, VMEM, VMEM],
        shape((near, far, W32, B), BF),
        [pltpu.VMEM((near, far, W32, B), F32)],
    )(tile_rows, tile_live, features.T, tiles)
    near_recv = lax.all_to_all(sent.reshape(near, far * W32, B), NEAR, 0, 0, tiled=True)

    far_part = call(
        functools.partial(near_kernel, q),
        [SMEM] + [VMEM] * 3,
        shape((far, q * W32 + slots, B), BF),
    )(place, near_recv, pos_t, neg_t)
    recv = lax.all_to_all(far_part, FAR, 0, 0, tiled=True)
    own = call(
        functools.partial(aggregate_kernel, q), [SMEM, VMEM], shape((q * (W32 + slots), B), BF)
    )(place, recv)
    blocks = lax.all_gather(own, REP, axis=0)

    nodes, agg, emb_t, slab_part = call(
        functools.partial(embed_kernel, q),
        [SMEM] + [VMEM] * 4,
        (
            shape((q * B, F), BF),
            shape((q, F, B), BF),
            shape((W32, B), BF),
            shape((xy, W32 + 2 * slots, B), BF),
        ),
        [pltpu.VMEM((q, F, B), BF)],
    )(place, blocks, weight, pos_t, neg_t)
    slab = lax.all_to_all(slab_part, COLUMN, 0, 0, tiled=True)
    cpos, ctot = call(
        functools.partial(direct_kernel, q, xy, slots),
        [SMEM, VMEM],
        (shape((groups, q * B, B), BF), shape((groups, q * B, B), BF)),
        [pltpu.VMEM((B, B), F32), pltpu.VMEM((slots, B, B), F32)],
        flops=100000000,
    )(place, blocks)

    pieces = call(
        functools.partial(decoder_kernel, q, xy, slots),
        [SMEM] + [VMEM] * 6,
        shape((q * q, W32 + 2 * W32 // q, B), BF),
        [
            pltpu.VMEM((groups, q * B, B), F32),
            pltpu.VMEM((groups, q * B, B), BF),
            pltpu.VMEM((groups, q * B, B), BF),
        ],
    )(place, slab, nodes, agg, weight, cpos, ctot)
    mine = lax.all_to_all(pieces, ("zh",) + REP, 0, 0, tiled=True)

    height = pieces.shape[1]
    far_part = call(functools.partial(owner_kernel, q), [VMEM], shape((far, height, B), BF))(mine)
    lines = lax.all_to_all(far_part, FAR, 0, 0, tiled=True)
    near_part = call(
        functools.partial(merge_kernel, q), [VMEM], shape((near, (far + 2) * W32, B), BF)
    )(lines)
    every = lax.all_to_all(near_part, NEAR, 0, 0, tiled=True)

    gf_t, grad_weight = call(
        functools.partial(features_kernel, q, nx, nh, nl),
        [SMEM, SMEM, VMEM, VMEM],
        (shape((W32, B), BF), shape((W32, F), F32)),
    )(tile_rows, tile_live, every, tiles)
    return (emb_t.T, grad_weight, gf_t.T)


def sharded(mesh):
    return jax.shard_map(
        on_device,
        mesh=mesh,
        in_specs=(
            P(ROWS, REP),
            P(),
            P(ROWS, None, None, None),
            P(ROWS, None),
            P(ROWS, None),
            P(ROWS, None),
            P(ROWS, None),
        ),
        out_specs=(P(ROWS, REP), P(REP, None), P(ROWS, REP)),
        check_vma=False,
    )


def solution(mesh):
    rows = mesh.shape["rows"]
    parts = mesh.devices.reshape(4, 4, rows // 32, 2, 2, 2)
    return sharded(Mesh(parts, ROWS + REP))
```

```python
import functools
import math

import jax
import jax.numpy as jnp
from jax import lax
from jax.experimental import pallas as pl
from jax.experimental.pallas import tpu as pltpu
from jax.sharding import Mesh, PartitionSpec as P

BF = jnp.bfloat16
F32 = jnp.float32
B = 128
F = 128
W32 = 32
NEAR = ("x", "yl")
FAR = ("zh", "yh")
COLUMN = ("x", "yh", "yl")
ROWS = ("zh",) + COLUMN
REP = ("zl", "core")
PARAMS = pltpu.CompilerParams(vmem_limit_bytes=40 * 1024 * 1024)
VMEM = pl.BlockSpec(memory_space=pltpu.VMEM)
SMEM = pl.BlockSpec(memory_space=pltpu.SMEM)


def tn(a, b):
    return lax.dot_general(a, b, (((0,), (0,)), ((), ())), preferred_element_type=F32)


def nt(a, b):
    return lax.dot_general(a, b, (((1,), (1,)), ((), ())), preferred_element_type=F32)


def nn(a, b):
    return lax.dot_general(a, b, (((1,), (0,)), ((), ())), preferred_element_type=F32)


def call(body, in_specs, out_shape, scratch=(), flops=1000000, nbytes=1000000):
    multi = isinstance(out_shape, (tuple, list))
    return pl.pallas_call(
        body,
        out_shape=out_shape,
        in_specs=in_specs,
        out_specs=[VMEM] * len(out_shape) if multi else VMEM,
        scratch_shapes=list(scratch),
        compiler_params=PARAMS,
        cost_estimate=pl.CostEstimate(flops=flops, bytes_accessed=nbytes, transcendentals=0),
    )


def split(value):
    high = value.astype(BF).astype(F32)
    return high, value - high


def products_kernel(nx, nh, nl, rows_ref, live_ref, feat_ref, tiles_ref, out_ref, acc):
    out_ref[...] = jnp.zeros_like(out_ref)
    slots = tiles_ref.shape[1]
    places = []
    for s in range(slots):
        row = rows_ref[0, s]
        plane, column = lax.div(row, nx * nh * nl), lax.rem(row, nx * nh * nl)
        line, place = lax.div(column, nh * nl), lax.rem(column, nh * nl)
        near = line * nl + lax.rem(place, nl)
        places.append((near, plane * nh + lax.div(place, nl)))
        acc[places[s]] = jnp.zeros((W32, B), F32)
    for s in range(slots):
        acc[places[s]] += nt(feat_ref[...], tiles_ref[0, s]) * live_ref[0, s].astype(F32)
    for s in range(slots):
        out_ref[places[s]] = acc[places[s]].astype(BF)


def near_kernel(recv_ref, out_ref):
    total = recv_ref[0].astype(F32)
    for r in range(1, recv_ref.shape[0]):
        total = total + recv_ref[r].astype(F32)
    out_ref[...] = total.astype(BF)


def aggregate_kernel(place_ref, recv_ref, pos_ref, neg_ref, out_ref):
    total = recv_ref[0].astype(F32)
    for r in range(1, recv_ref.shape[0]):
        total = total + recv_ref[r].astype(F32)
    total = total.astype(BF)
    ids = jnp.concatenate([pos_ref[...], neg_ref[...]], axis=0)
    block = lax.shift_right_logical(ids, 7)
    table = jnp.where(lax.rem(place_ref[0], 2) == 0, block, ids - block * B).astype(F32).astype(BF)
    for d in range(out_ref.shape[0]):
        out_ref[d, 0:W32, :] = total
        out_ref[d, W32:, :] = table


def embed_kernel(
    q, place_ref, got_ref, w_ref, pos_ref, neg_ref, nodes_ref, agg_ref, embt_ref, send_ref, et_s
):
    part, plane, column = place_ref[0], place_ref[1], place_ref[2]
    for b in range(q):
        for p in range(q):
            agg_ref[b, p * W32 : (p + 1) * W32, :] = got_ref[b * q + p, 0:W32, :]
        et = tn(w_ref[...], agg_ref[b])
        et_s[b] = et.astype(BF)
        nodes_ref[b * B : (b + 1) * B, :] = et.T.astype(BF)
    embt_ref[...] = et_s[plane, pl.ds(pl.multiple_of(part * W32, W32), W32), :]
    nodes = nodes_ref[pl.ds(pl.multiple_of(plane * B + part * W32, W32), W32), :]
    ids = jnp.concatenate([pos_ref[...], neg_ref[...]], axis=0)
    block = lax.shift_right_logical(ids, 7)
    table = jnp.concatenate([block, ids - block * B], axis=0).astype(F32)
    lane = lax.broadcasted_iota(jnp.int32, table.shape, 1)
    first = part * W32
    table = jnp.where((lane >= first) & (lane < first + W32), table, 0.0)
    quarters = B // W32
    turn = lax.rem(lax.rem(column, quarters) - part + quarters, quarters) * W32
    partners = pltpu.roll(table, turn, 1).astype(BF)
    for d in range(send_ref.shape[0]):
        send_ref[d, 0:W32, :] = nodes
        send_ref[d, W32:, :] = partners


def direct_kernel(q, xy, slots, place_ref, got_ref, cpos_ref, ctot_ref, want_s, wide_s):
    part, plane = place_ref[0], place_ref[1]
    pk = slots // 2
    lane = lax.broadcasted_iota(jnp.int32, (B, B), 1).astype(F32)
    first_block = (plane * xy).astype(F32)
    first_place = (part * W32).astype(F32)
    for d in range(q):
        piece = got_ref[d * q, W32:, :].astype(F32) - first_block
        place = got_ref[d * q + 1, W32:, :].astype(F32) - first_place
        inside = (piece >= 0.0) & (piece < float(xy)) & (place >= 0.0) & (place < float(W32))
        want = jnp.where(inside, piece * W32 + place, -1.0)
        want_s[...] = jnp.concatenate([want, jnp.zeros((B - slots, B), F32)], axis=0).T
        for k in range(slots):
            wide_s[k] = jnp.broadcast_to(want_s[:, k : k + 1], (B, B))

        def step(g, carry):
            at = lane + (g * B).astype(F32)
            cpos = jnp.zeros((B, B), F32)
            cneg = jnp.zeros((B, B), F32)
            for k in range(pk):
                cpos = jnp.where(wide_s[k] == at, cpos + 1.0, cpos)
                cneg = jnp.where(wide_s[pk + k] == at, cneg + 1.0, cneg)
            cpos_ref[g, d * B : (d + 1) * B, :] = cpos.astype(BF)
            ctot_ref[g, d * B : (d + 1) * B, :] = (cpos + cneg).astype(BF)
            return carry

        lax.fori_loop(0, cpos_ref.shape[0], step, 0)


def decoder_kernel(
    q, xy, slots, place_ref, got_ref, en_ref, agg_ref, w_ref, cpos_ref, ctot_ref,
    out_ref, logit_s, high_s, low_s,
):
    pk = slots // 2
    column = place_ref[2]
    quarters = B // W32
    groups = got_ref.shape[0] // quarters
    tile = 16
    sub = [
        (lax.broadcasted_iota(jnp.int32, (tile, B), 0) + i * tile).astype(F32).astype(BF)
        for i in range(B // tile)
    ]
    en = en_ref[...]
    for g in range(groups):
        em = got_ref[g * quarters : (g + 1) * quarters, 0:W32, :].reshape(B, F)
        logit_s[g] = nt(en, em)
    half = 0.5 / math.sqrt(F)
    one, zero = jnp.ones((tile, B), BF), jnp.zeros((tile, B), BF)

    def step(g, carry):
        table = got_ref[g * quarters, W32:, :].astype(F32)
        for j in range(1, quarters):
            table = table + got_ref[g * quarters + j, W32:, :].astype(F32)
        for d in range(q):
            block = d * xy + column
            code = jnp.where(table[:slots] == block.astype(F32), table[slots:], -1.0)
            wide = [
                jnp.broadcast_to(code[k : k + 1], (tile, B)).astype(BF) for k in range(slots)
            ]
            both, ineg = [], []
            for i in range(B // tile):
                cp, cn = zero, zero
                for k in range(pk):
                    cp = jnp.where(wide[k] == sub[i], cp + one, cp)
                    cn = jnp.where(wide[pk + k] == sub[i], cn + one, cn)
                both.append(cp)
                ineg.append(cp + cn)
            rows = slice(d * B, (d + 1) * B)
            cpos = (cpos_ref[g, rows, :] + jnp.concatenate(both, axis=0)).astype(F32)
            ctot = (ctot_ref[g, rows, :] + jnp.concatenate(ineg, axis=0)).astype(F32)
            sig = 0.5 * jnp.tanh(logit_s[g, rows, :] * half) + 0.5
            high, low = split(ctot * sig - cpos)
            high_s[g, rows, :] = high.astype(BF)
            low_s[g, rows, :] = low.astype(BF)
        return carry

    lax.fori_loop(0, groups, step, 0)
    grad = jnp.zeros((q * B, F), F32)
    for g in range(groups):
        em = got_ref[g * quarters : (g + 1) * quarters, 0:W32, :].reshape(B, F)
        grad = grad + nn(high_s[g], em) + nn(low_s[g], em)
    high, low = split(grad * (1.0 / pk))
    high, low = high.astype(BF), low.astype(BF)
    grad_agg = nt(w_ref[...], high) + nt(w_ref[...], low)
    terms = jnp.zeros((F, F), F32)
    for d in range(q):
        rows = slice(d * B, (d + 1) * B)
        terms = terms + nn(agg_ref[d], high[rows]) + nn(agg_ref[d], low[rows])
    thigh, tlow = split(terms)
    eighth = W32 // q
    for z in range(q):
        for p in range(q):
            cols = grad_agg[p * W32 : (p + 1) * W32, z * B : (z + 1) * B]
            out_ref[z * q + p, 0:W32, :] = cols.astype(BF)
            first = p * W32 + z * eighth
            piece = [thigh[first : first + eighth], tlow[first : first + eighth]]
            out_ref[z * q + p, W32:, :] = jnp.concatenate(piece, axis=0).astype(BF)


def owner_kernel(q, got_ref, out_ref):
    total = got_ref[0].astype(F32)
    for r in range(1, got_ref.shape[0]):
        total = total + got_ref[r].astype(F32)
    eighth = W32 // q
    high, low = split(total[W32 : W32 + eighth] + total[W32 + eighth :])
    sent = jnp.concatenate([total[:W32], high, low], axis=0).astype(BF)
    for d in range(out_ref.shape[0]):
        out_ref[d] = sent


def merge_kernel(q, got_ref, out_ref):
    count = got_ref.shape[0]
    nh = count // q
    eighth = W32 // q
    blocks = got_ref[:, 0:W32, :].reshape(count * W32, B)
    rows = []
    for z in range(q):
        total = got_ref[z * nh, W32:, :].astype(F32)
        for h in range(1, nh):
            total = total + got_ref[z * nh + h, W32:, :].astype(F32)
        rows.append(total[:eighth] + total[eighth:])
    terms = jnp.concatenate(rows, axis=0).astype(BF)
    for d in range(out_ref.shape[0]):
        out_ref[d, 0 : count * W32, :] = blocks
        out_ref[d, count * W32 :, :] = terms


def features_kernel(q, nx, nh, nl, rows_ref, live_ref, got_ref, tiles_ref, gft_ref, gw_ref):
    total = jnp.zeros((W32, B), F32)
    for s in range(tiles_ref.shape[1]):
        row = rows_ref[0, s]
        plane, column = lax.div(row, nx * nh * nl), lax.rem(row, nx * nh * nl)
        line, place = lax.div(column, nh * nl), lax.rem(column, nh * nl)
        near = line * nl + lax.rem(place, nl)
        first = pl.multiple_of((plane * nh + lax.div(place, nl)) * W32, W32)
        live = live_ref[0, s].astype(F32)
        block = got_ref[near, pl.ds(first, W32), :].astype(F32) * live
        total = total + nn(block.astype(BF), tiles_ref[0, s])
    gft_ref[...] = total.astype(BF)
    first = q * nh * W32
    terms = got_ref[:, first:, :].astype(F32)
    gw_ref[...] = jnp.sum(terms, axis=0) * (1.0 / math.sqrt(q * nx * nh * nl * B))


def on_device(features, weight, tiles, tile_rows, tile_live, pos_partner, neg_partner):
    q, nx = lax.axis_size("zh"), lax.axis_size("x")
    nh, nl = lax.axis_size("yh"), lax.axis_size("yl")
    xy, near, far = nx * nh * nl, nx * nl, q * nh
    axes = (REP, "zh", COLUMN)
    place = jnp.stack([lax.axis_index(axis) for axis in axes]).astype(jnp.int32)
    shape = jax.ShapeDtypeStruct
    slots = 2 * pos_partner.shape[1]
    groups = xy * W32 // B
    pos_t, neg_t = pos_partner.T, neg_partner.T

    sent = call(
        functools.partial(products_kernel, nx, nh, nl),
        [SMEM, SMEM, VMEM, VMEM],
        shape((near, far, W32, B), BF),
        [pltpu.VMEM((near, far, W32, B), F32)],
    )(tile_rows, tile_live, features.T, tiles)
    near_recv = lax.all_to_all(sent.reshape(near, far * W32, B), NEAR, 0, 0, tiled=True)

    near_sum = call(near_kernel, [VMEM], shape((far * W32, B), BF))(near_recv)
    recv = lax.all_to_all(near_sum.reshape(far, W32, B), FAR, 0, 0, tiled=True)
    own = call(
        aggregate_kernel, [SMEM] + [VMEM] * 3, shape((q * q, W32 + slots, B), BF)
    )(place, recv, pos_t, neg_t)
    blocks = lax.all_to_all(own, ("zh",) + REP, 0, 0, tiled=True)

    nodes, agg, emb_t, slab_part = call(
        functools.partial(embed_kernel, q),
        [SMEM] + [VMEM] * 4,
        (
            shape((q * B, F), BF),
            shape((q, F, B), BF),
            shape((W32, B), BF),
            shape((xy, W32 + 2 * slots, B), BF),
        ),
        [pltpu.VMEM((q, F, B), BF)],
    )(place, blocks, weight, pos_t, neg_t)
    slab = lax.all_to_all(slab_part, COLUMN, 0, 0, tiled=True)
    cpos, ctot = call(
        functools.partial(direct_kernel, q, xy, slots),
        [SMEM, VMEM],
        (shape((groups, q * B, B), BF), shape((groups, q * B, B), BF)),
        [pltpu.VMEM((B, B), F32), pltpu.VMEM((slots, B, B), F32)],
        flops=100000000,
    )(place, blocks)

    pieces = call(
        functools.partial(decoder_kernel, q, xy, slots),
        [SMEM] + [VMEM] * 6,
        shape((q * q, W32 + 2 * W32 // q, B), BF),
        [
            pltpu.VMEM((groups, q * B, B), F32),
            pltpu.VMEM((groups, q * B, B), BF),
            pltpu.VMEM((groups, q * B, B), BF),
        ],
    )(place, slab, nodes, agg, weight, cpos, ctot)
    mine = lax.all_to_all(pieces, ("zh",) + REP, 0, 0, tiled=True)

    height = pieces.shape[1]
    far_part = call(functools.partial(owner_kernel, q), [VMEM], shape((far, height, B), BF))(mine)
    lines = lax.all_to_all(far_part, FAR, 0, 0, tiled=True)
    near_part = call(
        functools.partial(merge_kernel, q), [VMEM], shape((near, (far + 1) * W32, B), BF)
    )(lines)
    every = lax.all_to_all(near_part, NEAR, 0, 0, tiled=True)

    gf_t, grad_weight = call(
        functools.partial(features_kernel, q, nx, nh, nl),
        [SMEM, SMEM, VMEM, VMEM],
        (shape((W32, B), BF), shape((W32, F), F32)),
    )(tile_rows, tile_live, every, tiles)
    return (emb_t.T, grad_weight, gf_t.T)


def sharded(mesh):
    return jax.shard_map(
        on_device,
        mesh=mesh,
        in_specs=(
            P(ROWS, REP),
            P(),
            P(ROWS, None, None, None),
            P(ROWS, None),
            P(ROWS, None),
            P(ROWS, None),
            P(ROWS, None),
        ),
        out_specs=(P(ROWS, REP), P(REP, None), P(ROWS, REP)),
        check_vma=False,
    )


def solution(mesh):
    rows = mesh.shape["rows"]
    parts = mesh.devices.reshape(4, 4, rows // 32, 2, 2, 2)
    return sharded(Mesh(parts, ROWS + REP))
```

```python
import functools
import math

import jax
import jax.numpy as jnp
from jax import lax
from jax.experimental import pallas as pl
from jax.experimental.pallas import tpu as pltpu
from jax.sharding import Mesh, PartitionSpec as P

BF = jnp.bfloat16
F32 = jnp.float32
B = 128
F = 128
W32 = 32
NEAR = ("x", "yl")
FAR = ("zh", "yh")
COLUMN = ("x", "yh", "yl")
ROWS = ("zh",) + COLUMN
REP = ("zl", "core")
PARAMS = pltpu.CompilerParams(vmem_limit_bytes=40 * 1024 * 1024)
VMEM = pl.BlockSpec(memory_space=pltpu.VMEM)
SMEM = pl.BlockSpec(memory_space=pltpu.SMEM)


def tn(a, b):
    return lax.dot_general(a, b, (((0,), (0,)), ((), ())), preferred_element_type=F32)


def nt(a, b):
    return lax.dot_general(a, b, (((1,), (1,)), ((), ())), preferred_element_type=F32)


def nn(a, b):
    return lax.dot_general(a, b, (((1,), (0,)), ((), ())), preferred_element_type=F32)


def call(body, in_specs, out_shape, scratch=(), flops=1000000, nbytes=1000000):
    multi = isinstance(out_shape, (tuple, list))
    return pl.pallas_call(
        body,
        out_shape=out_shape,
        in_specs=in_specs,
        out_specs=[VMEM] * len(out_shape) if multi else VMEM,
        scratch_shapes=list(scratch),
        compiler_params=PARAMS,
        cost_estimate=pl.CostEstimate(flops=flops, bytes_accessed=nbytes, transcendentals=0),
    )


def split(value):
    high = value.astype(BF).astype(F32)
    return high, value - high


def products_kernel(nx, nh, nl, rows_ref, live_ref, feat_ref, tiles_ref, out_ref, acc):
    out_ref[...] = jnp.zeros_like(out_ref)
    slots = tiles_ref.shape[1]
    places = []
    for s in range(slots):
        row = rows_ref[0, s]
        plane, column = lax.div(row, nx * nh * nl), lax.rem(row, nx * nh * nl)
        line, place = lax.div(column, nh * nl), lax.rem(column, nh * nl)
        near = line * nl + lax.rem(place, nl)
        places.append((near, plane * nh + lax.div(place, nl)))
        acc[places[s]] = jnp.zeros((W32, B), F32)
    for s in range(slots):
        acc[places[s]] += nt(feat_ref[...], tiles_ref[0, s]) * live_ref[0, s].astype(F32)
    for s in range(slots):
        out_ref[places[s]] = acc[places[s]].astype(BF)


def near_kernel(recv_ref, out_ref):
    total = recv_ref[0].astype(F32)
    for r in range(1, recv_ref.shape[0]):
        total = total + recv_ref[r].astype(F32)
    out_ref[...] = total.astype(BF)


def aggregate_kernel(place_ref, recv_ref, pos_ref, neg_ref, out_ref):
    total = recv_ref[0].astype(F32)
    for r in range(1, recv_ref.shape[0]):
        total = total + recv_ref[r].astype(F32)
    total = total.astype(BF)
    ids = jnp.concatenate([pos_ref[...], neg_ref[...]], axis=0)
    block = lax.shift_right_logical(ids, 7)
    table = jnp.where(lax.rem(place_ref[0], 2) == 0, block, ids - block * B).astype(F32).astype(BF)
    for d in range(out_ref.shape[0]):
        out_ref[d, 0:W32, :] = total
        out_ref[d, W32:, :] = table


def embed_kernel(
    q, place_ref, got_ref, w_ref, pos_ref, neg_ref, nodes_ref, agg_ref, embt_ref, send_ref, et_s
):
    part, plane, column = place_ref[0], place_ref[1], place_ref[2]
    for b in range(q):
        for p in range(q):
            agg_ref[b, p * W32 : (p + 1) * W32, :] = got_ref[b * q + p, 0:W32, :]
        et = tn(w_ref[...], agg_ref[b])
        et_s[b] = et.astype(BF)
        nodes_ref[b * B : (b + 1) * B, :] = et.T.astype(BF)
    embt_ref[...] = et_s[plane, pl.ds(pl.multiple_of(part * W32, W32), W32), :]
    nodes = nodes_ref[pl.ds(pl.multiple_of(plane * B + part * W32, W32), W32), :]
    ids = jnp.concatenate([pos_ref[...], neg_ref[...]], axis=0)
    block = lax.shift_right_logical(ids, 7)
    lane = lax.broadcasted_iota(jnp.int32, ids.shape, 1)
    first = part * W32
    mine = (lane >= first) & (lane < first + W32)
    blocks = jnp.where(mine, block, 0).astype(F32)
    places = jnp.where(mine, ids - block * B, 0).astype(F32)
    quarters = B // W32
    turn = lax.rem(lax.rem(column, quarters) - part + quarters, quarters) * W32
    partners = pltpu.roll(blocks + pltpu.roll(places, B // 2, 1), turn, 1).astype(BF)
    for d in range(send_ref.shape[0]):
        send_ref[d, 0:W32, :] = nodes
        send_ref[d, W32:, :] = partners


def direct_kernel(q, xy, slots, place_ref, got_ref, cpos_ref, ctot_ref, want_s, wide_s):
    part, plane = place_ref[0], place_ref[1]
    pk = slots // 2
    lane = lax.broadcasted_iota(jnp.int32, (B, B), 1).astype(F32)
    first_block = (plane * xy).astype(F32)
    first_place = (part * W32).astype(F32)
    for d in range(q):
        piece = got_ref[d * q, W32:, :].astype(F32) - first_block
        place = got_ref[d * q + 1, W32:, :].astype(F32) - first_place
        inside = (piece >= 0.0) & (piece < float(xy)) & (place >= 0.0) & (place < float(W32))
        want = jnp.where(inside, piece * W32 + place, -1.0)
        want_s[...] = jnp.concatenate([want, jnp.zeros((B - slots, B), F32)], axis=0).T
        for k in range(slots):
            wide_s[k] = jnp.broadcast_to(want_s[:, k : k + 1], (B, B))

        def step(g, carry):
            at = lane + (g * B).astype(F32)
            cpos = jnp.zeros((B, B), F32)
            cneg = jnp.zeros((B, B), F32)
            for k in range(pk):
                cpos = jnp.where(wide_s[k] == at, cpos + 1.0, cpos)
                cneg = jnp.where(wide_s[pk + k] == at, cneg + 1.0, cneg)
            cpos_ref[g, d * B : (d + 1) * B, :] = cpos.astype(BF)
            ctot_ref[g, d * B : (d + 1) * B, :] = (cpos + cneg).astype(BF)
            return carry

        lax.fori_loop(0, cpos_ref.shape[0], step, 0)


def decoder_kernel(
    q, xy, slots, place_ref, got_ref, en_ref, agg_ref, w_ref, cpos_ref, ctot_ref,
    out_ref, logit_s, coef_s,
):
    pk = slots // 2
    column = place_ref[2]
    quarters = B // W32
    groups = got_ref.shape[0] // quarters
    tile = 16
    sub = [
        (lax.broadcasted_iota(jnp.int32, (tile, B), 0) + i * tile).astype(F32).astype(BF)
        for i in range(B // tile)
    ]
    en = en_ref[...]
    for g in range(groups):
        em = got_ref[g * quarters : (g + 1) * quarters, 0:W32, :].reshape(B, F)
        logit_s[g] = nt(en, em)
    quarter = lax.div(lax.broadcasted_iota(jnp.int32, (slots, B), 1), W32)
    half = 0.5 / math.sqrt(F)
    one, zero = jnp.ones((tile, B), BF), jnp.zeros((tile, B), BF)

    def step(g, carry):
        theirs = jnp.zeros((slots, B), F32)
        places = jnp.zeros((slots, B), F32)
        for j in range(quarters):
            table = got_ref[g * quarters + j, W32:, :].astype(F32)
            theirs = jnp.where(quarter == j, table, theirs)
            places = jnp.where(quarter == (j + quarters // 2) % quarters, table, places)
        places = pltpu.roll(places, B // 2, 1)
        for d in range(q):
            block = d * xy + column
            code = jnp.where(theirs == block.astype(F32), places, -1.0)
            wide = [
                jnp.broadcast_to(code[k : k + 1], (tile, B)).astype(BF) for k in range(slots)
            ]
            both, ineg = [], []
            for i in range(B // tile):
                cp, cn = zero, zero
                for k in range(pk):
                    cp = jnp.where(wide[k] == sub[i], cp + one, cp)
                    cn = jnp.where(wide[pk + k] == sub[i], cn + one, cn)
                both.append(cp)
                ineg.append(cp + cn)
            rows = slice(d * B, (d + 1) * B)
            cpos = (cpos_ref[g, rows, :] + jnp.concatenate(both, axis=0)).astype(F32)
            ctot = (ctot_ref[g, rows, :] + jnp.concatenate(ineg, axis=0)).astype(F32)
            sig = 0.5 * jnp.tanh(logit_s[g, rows, :] * half) + 0.5
            coef_s[g, rows, :] = (ctot * sig - cpos).astype(BF)
        return carry

    lax.fori_loop(0, groups, step, 0)
    grad = jnp.zeros((q * B, F), F32)
    for g in range(groups):
        em = got_ref[g * quarters : (g + 1) * quarters, 0:W32, :].reshape(B, F)
        grad = grad + nn(coef_s[g], em)
    high, low = split(grad * (1.0 / pk))
    high, low = high.astype(BF), low.astype(BF)
    grad_agg = nt(w_ref[...], high) + nt(w_ref[...], low)
    terms = jnp.zeros((F, F), F32)
    for d in range(q):
        rows = slice(d * B, (d + 1) * B)
        terms = terms + nn(agg_ref[d], high[rows]) + nn(agg_ref[d], low[rows])
    thigh, tlow = split(terms)
    eighth = W32 // q
    for z in range(q):
        for p in range(q):
            cols = grad_agg[p * W32 : (p + 1) * W32, z * B : (z + 1) * B]
            out_ref[z * q + p, 0:W32, :] = cols.astype(BF)
            first = p * W32 + z * eighth
            piece = [thigh[first : first + eighth], tlow[first : first + eighth]]
            out_ref[z * q + p, W32:, :] = jnp.concatenate(piece, axis=0).astype(BF)


def owner_kernel(q, got_ref, out_ref):
    total = got_ref[0].astype(F32)
    for r in range(1, got_ref.shape[0]):
        total = total + got_ref[r].astype(F32)
    eighth = W32 // q
    high, low = split(total[W32 : W32 + eighth] + total[W32 + eighth :])
    sent = jnp.concatenate([total[:W32], high, low], axis=0).astype(BF)
    for d in range(out_ref.shape[0]):
        out_ref[d] = sent


def merge_kernel(q, got_ref, out_ref):
    count = got_ref.shape[0]
    nh = count // q
    eighth = W32 // q
    blocks = got_ref[:, 0:W32, :].reshape(count * W32, B)
    rows = []
    for z in range(q):
        total = got_ref[z * nh, W32:, :].astype(F32)
        for h in range(1, nh):
            total = total + got_ref[z * nh + h, W32:, :].astype(F32)
        rows.append(total[:eighth] + total[eighth:])
    terms = jnp.concatenate(rows, axis=0).astype(BF)
    for d in range(out_ref.shape[0]):
        out_ref[d, 0 : count * W32, :] = blocks
        out_ref[d, count * W32 :, :] = terms


def features_kernel(q, nx, nh, nl, rows_ref, live_ref, got_ref, tiles_ref, gft_ref, gw_ref):
    slots = tiles_ref.shape[1]
    blocks = []
    for s in range(slots):
        row = rows_ref[0, s]
        plane, column = lax.div(row, nx * nh * nl), lax.rem(row, nx * nh * nl)
        line, place = lax.div(column, nh * nl), lax.rem(column, nh * nl)
        near = line * nl + lax.rem(place, nl)
        first = pl.multiple_of((plane * nh + lax.div(place, nl)) * W32, W32)
        live = live_ref[0, s].astype(F32)
        blocks.append((got_ref[near, pl.ds(first, W32), :].astype(F32) * live).astype(BF))
    total = nn(jnp.concatenate(blocks, axis=1), tiles_ref[0].reshape(slots * B, B))
    gft_ref[...] = total.astype(BF)
    first = q * nh * W32
    terms = got_ref[:, first:, :].astype(F32)
    gw_ref[...] = jnp.sum(terms, axis=0) * (1.0 / math.sqrt(q * nx * nh * nl * B))


def on_device(features, weight, tiles, tile_rows, tile_live, pos_partner, neg_partner):
    q, nx = lax.axis_size("zh"), lax.axis_size("x")
    nh, nl = lax.axis_size("yh"), lax.axis_size("yl")
    xy, near, far = nx * nh * nl, nx * nl, q * nh
    axes = (REP, "zh", COLUMN)
    place = jnp.stack([lax.axis_index(axis) for axis in axes]).astype(jnp.int32)
    shape = jax.ShapeDtypeStruct
    slots = 2 * pos_partner.shape[1]
    groups = xy * W32 // B
    pos_t, neg_t = pos_partner.T, neg_partner.T

    sent = call(
        functools.partial(products_kernel, nx, nh, nl),
        [SMEM, SMEM, VMEM, VMEM],
        shape((near, far, W32, B), BF),
        [pltpu.VMEM((near, far, W32, B), F32)],
    )(tile_rows, tile_live, features.T, tiles)
    near_recv = lax.all_to_all(sent.reshape(near, far * W32, B), NEAR, 0, 0, tiled=True)

    near_sum = call(near_kernel, [VMEM], shape((far * W32, B), BF))(near_recv)
    recv = lax.all_to_all(near_sum.reshape(far, W32, B), FAR, 0, 0, tiled=True)
    own = call(
        aggregate_kernel, [SMEM] + [VMEM] * 3, shape((q * q, W32 + slots, B), BF)
    )(place, recv, pos_t, neg_t)
    blocks = lax.all_to_all(own, ("zh",) + REP, 0, 0, tiled=True)

    nodes, agg, emb_t, slab_part = call(
        functools.partial(embed_kernel, q),
        [SMEM] + [VMEM] * 4,
        (
            shape((q * B, F), BF),
            shape((q, F, B), BF),
            shape((W32, B), BF),
            shape((xy, W32 + slots, B), BF),
        ),
        [pltpu.VMEM((q, F, B), BF)],
    )(place, blocks, weight, pos_t, neg_t)
    slab = lax.all_to_all(slab_part, COLUMN, 0, 0, tiled=True)
    cpos, ctot = call(
        functools.partial(direct_kernel, q, xy, slots),
        [SMEM, VMEM],
        (shape((groups, q * B, B), BF), shape((groups, q * B, B), BF)),
        [pltpu.VMEM((B, B), F32), pltpu.VMEM((slots, B, B), F32)],
        flops=100000000,
    )(place, blocks)

    pieces = call(
        functools.partial(decoder_kernel, q, xy, slots),
        [SMEM] + [VMEM] * 6,
        shape((q * q, W32 + 2 * W32 // q, B), BF),
        [
            pltpu.VMEM((groups, q * B, B), F32),
            pltpu.VMEM((groups, q * B, B), BF),
        ],
    )(place, slab, nodes, agg, weight, cpos, ctot)
    mine = lax.all_to_all(pieces, ("zh",) + REP, 0, 0, tiled=True)

    height = pieces.shape[1]
    far_part = call(functools.partial(owner_kernel, q), [VMEM], shape((far, height, B), BF))(mine)
    lines = lax.all_to_all(far_part, FAR, 0, 0, tiled=True)
    near_part = call(
        functools.partial(merge_kernel, q), [VMEM], shape((near, (far + 1) * W32, B), BF)
    )(lines)
    every = lax.all_to_all(near_part, NEAR, 0, 0, tiled=True)

    gf_t, grad_weight = call(
        functools.partial(features_kernel, q, nx, nh, nl),
        [SMEM, SMEM, VMEM, VMEM],
        (shape((W32, B), BF), shape((W32, F), F32)),
    )(tile_rows, tile_live, every, tiles)
    return (emb_t.T, grad_weight, gf_t.T)


def sharded(mesh):
    return jax.shard_map(
        on_device,
        mesh=mesh,
        in_specs=(
            P(ROWS, REP),
            P(),
            P(ROWS, None, None, None),
            P(ROWS, None),
            P(ROWS, None),
            P(ROWS, None),
            P(ROWS, None),
        ),
        out_specs=(P(ROWS, REP), P(REP, None), P(ROWS, REP)),
        check_vma=False,
    )


def solution(mesh):
    rows = mesh.shape["rows"]
    parts = mesh.devices.reshape(4, 4, rows // 32, 2, 2, 2)
    return sharded(Mesh(parts, ROWS + REP))
```

```python
import functools
import math

import jax
import jax.numpy as jnp
from jax import lax
from jax.experimental import pallas as pl
from jax.experimental.pallas import tpu as pltpu
from jax.sharding import Mesh, PartitionSpec as P

BF = jnp.bfloat16
F32 = jnp.float32
B = 128
F = 128
W32 = 32
NEAR = ("x", "yl")
FAR = ("zh", "yh")
COLUMN = ("x", "yh", "yl")
ROWS = ("zh",) + COLUMN
REP = ("zl", "core")
PARAMS = pltpu.CompilerParams(vmem_limit_bytes=40 * 1024 * 1024)
VMEM = pl.BlockSpec(memory_space=pltpu.VMEM)
SMEM = pl.BlockSpec(memory_space=pltpu.SMEM)


def tn(a, b):
    return lax.dot_general(a, b, (((0,), (0,)), ((), ())), preferred_element_type=F32)


def nt(a, b):
    return lax.dot_general(a, b, (((1,), (1,)), ((), ())), preferred_element_type=F32)


def nn(a, b):
    return lax.dot_general(a, b, (((1,), (0,)), ((), ())), preferred_element_type=F32)


def call(body, in_specs, out_shape, scratch=(), flops=1000000, nbytes=1000000, params=PARAMS):
    multi = isinstance(out_shape, (tuple, list))
    return pl.pallas_call(
        body,
        out_shape=out_shape,
        in_specs=in_specs,
        out_specs=[VMEM] * len(out_shape) if multi else VMEM,
        scratch_shapes=list(scratch),
        compiler_params=params,
        cost_estimate=pl.CostEstimate(flops=flops, bytes_accessed=nbytes, transcendentals=0),
    )


def split(value):
    high = value.astype(BF).astype(F32)
    return high, value - high


def products_kernel(nx, nh, nl, rows_ref, live_ref, feat_ref, tiles_ref, out_ref, acc):
    out_ref[...] = jnp.zeros_like(out_ref)
    slots = tiles_ref.shape[1]
    places = []
    for s in range(slots):
        row = rows_ref[0, s]
        plane, column = lax.div(row, nx * nh * nl), lax.rem(row, nx * nh * nl)
        line, place = lax.div(column, nh * nl), lax.rem(column, nh * nl)
        near = line * nl + lax.rem(place, nl)
        places.append((near, plane * nh + lax.div(place, nl)))
        acc[places[s]] = jnp.zeros((W32, B), F32)
    for s in range(slots):
        acc[places[s]] += nt(feat_ref[...], tiles_ref[0, s]) * live_ref[0, s].astype(F32)
    for s in range(slots):
        out_ref[places[s]] = acc[places[s]].astype(BF)


def near_kernel(recv_ref, out_ref):
    total = recv_ref[0].astype(F32)
    for r in range(1, recv_ref.shape[0]):
        total = total + recv_ref[r].astype(F32)
    out_ref[...] = total.astype(BF)


def aggregate_kernel(place_ref, recv_ref, pos_ref, neg_ref, out_ref):
    total = recv_ref[0].astype(F32)
    for r in range(1, recv_ref.shape[0]):
        total = total + recv_ref[r].astype(F32)
    total = total.astype(BF)
    ids = jnp.concatenate([pos_ref[...], neg_ref[...]], axis=0)
    block = lax.shift_right_logical(ids, 7)
    table = jnp.where(lax.rem(place_ref[0], 2) == 0, block, ids - block * B).astype(F32).astype(BF)
    for d in range(out_ref.shape[0]):
        out_ref[d, 0:W32, :] = total
        out_ref[d, W32:, :] = table


def embed_kernel(
    q, place_ref, got_ref, w_ref, pos_ref, neg_ref, nodes_ref, agg_ref, embt_ref, send_ref, et_s
):
    part, plane, column = place_ref[0], place_ref[1], place_ref[2]
    for b in range(q):
        for p in range(q):
            agg_ref[b, p * W32 : (p + 1) * W32, :] = got_ref[b * q + p, 0:W32, :]
        et = tn(w_ref[...], agg_ref[b])
        et_s[b] = et.astype(BF)
        nodes_ref[b * B : (b + 1) * B, :] = et.T.astype(BF)
    embt_ref[...] = et_s[plane, pl.ds(pl.multiple_of(part * W32, W32), W32), :]
    nodes = nodes_ref[pl.ds(pl.multiple_of(plane * B + part * W32, W32), W32), :]
    ids = jnp.concatenate([pos_ref[...], neg_ref[...]], axis=0)
    block = lax.shift_right_logical(ids, 7)
    lane = lax.broadcasted_iota(jnp.int32, ids.shape, 1)
    first = part * W32
    mine = (lane >= first) & (lane < first + W32)
    blocks = jnp.where(mine, block, 0).astype(F32)
    places = jnp.where(mine, ids - block * B, 0).astype(F32)
    quarters = B // W32
    turn = lax.rem(lax.rem(column, quarters) - part + quarters, quarters) * W32
    partners = pltpu.roll(blocks + pltpu.roll(places, B // 2, 1), turn, 1).astype(BF)
    for d in range(send_ref.shape[0]):
        send_ref[d, 0:W32, :] = nodes
        send_ref[d, W32:, :] = partners


def direct_kernel(q, xy, slots, place_ref, got_ref, cpos_ref, ctot_ref, want_s, wide_s):
    part, plane = place_ref[0], place_ref[1]
    pk = slots // 2
    lane = lax.broadcasted_iota(jnp.int32, (B, B), 1).astype(F32)
    first_block = (plane * xy).astype(F32)
    first_place = (part * W32).astype(F32)
    for d in range(q):
        piece = got_ref[d * q, W32:, :].astype(F32) - first_block
        place = got_ref[d * q + 1, W32:, :].astype(F32) - first_place
        inside = (piece >= 0.0) & (piece < float(xy)) & (place >= 0.0) & (place < float(W32))
        want = jnp.where(inside, piece * W32 + place, -1.0)
        want_s[...] = jnp.concatenate([want, jnp.zeros((B - slots, B), F32)], axis=0).T
        for k in range(slots):
            wide_s[k] = jnp.broadcast_to(want_s[:, k : k + 1], (B, B))

        def step(g, carry):
            at = lane + (g * B).astype(F32)
            cpos = jnp.zeros((B, B), F32)
            cneg = jnp.zeros((B, B), F32)
            for k in range(pk):
                cpos = jnp.where(wide_s[k] == at, cpos + 1.0, cpos)
                cneg = jnp.where(wide_s[pk + k] == at, cneg + 1.0, cneg)
            cpos_ref[g, d * B : (d + 1) * B, :] = cpos.astype(BF)
            ctot_ref[g, d * B : (d + 1) * B, :] = (cpos + cneg).astype(BF)
            return carry

        lax.fori_loop(0, cpos_ref.shape[0], step, 0)


def decoder_kernel(
    q, xy, slots, place_ref, got_ref, en_ref, agg_ref, w_ref, cpos_ref, ctot_ref,
    out_ref, logit_s, coef_s,
):
    pk = slots // 2
    column = place_ref[2]
    quarters = B // W32
    groups = got_ref.shape[0] // quarters
    tile = 16
    sub = [
        (lax.broadcasted_iota(jnp.int32, (tile, B), 0) + i * tile).astype(F32).astype(BF)
        for i in range(B // tile)
    ]
    en = en_ref[...]
    for g in range(groups):
        em = got_ref[g * quarters : (g + 1) * quarters, 0:W32, :].reshape(B, F)
        logit_s[g] = nt(en, em)
    quarter = lax.div(lax.broadcasted_iota(jnp.int32, (slots, B), 1), W32)
    half = 0.5 / math.sqrt(F)
    one, zero = jnp.ones((tile, B), BF), jnp.zeros((tile, B), BF)

    def step(g, carry):
        theirs = jnp.zeros((slots, B), F32)
        places = jnp.zeros((slots, B), F32)
        for j in range(quarters):
            table = got_ref[g * quarters + j, W32:, :].astype(F32)
            theirs = jnp.where(quarter == j, table, theirs)
            places = jnp.where(quarter == (j + quarters // 2) % quarters, table, places)
        places = pltpu.roll(places, B // 2, 1)
        for d in range(q):
            block = d * xy + column
            code = jnp.where(theirs == block.astype(F32), places, -1.0)
            wide = [
                jnp.broadcast_to(code[k : k + 1], (tile, B)).astype(BF) for k in range(slots)
            ]
            both, ineg = [], []
            for i in range(B // tile):
                cp, cn = zero, zero
                for k in range(pk):
                    cp = jnp.where(wide[k] == sub[i], cp + one, cp)
                    cn = jnp.where(wide[pk + k] == sub[i], cn + one, cn)
                both.append(cp)
                ineg.append(cp + cn)
            rows = slice(d * B, (d + 1) * B)
            cpos = (cpos_ref[g, rows, :] + jnp.concatenate(both, axis=0)).astype(F32)
            ctot = (ctot_ref[g, rows, :] + jnp.concatenate(ineg, axis=0)).astype(F32)
            sig = 0.5 * jnp.tanh(logit_s[g, rows, :] * half) + 0.5
            coef_s[g, rows, :] = (ctot * sig - cpos).astype(BF)
        return carry

    lax.fori_loop(0, groups, step, 0)
    grad = jnp.zeros((q * B, F), F32)
    for g in range(groups):
        em = got_ref[g * quarters : (g + 1) * quarters, 0:W32, :].reshape(B, F)
        grad = grad + nn(coef_s[g], em)
    high, low = split(grad * (1.0 / pk))
    high, low = high.astype(BF), low.astype(BF)
    grad_agg = nt(w_ref[...], high) + nt(w_ref[...], low)
    terms = jnp.zeros((F, F), F32)
    for d in range(q):
        rows = slice(d * B, (d + 1) * B)
        terms = terms + nn(agg_ref[d], high[rows]) + nn(agg_ref[d], low[rows])
    thigh, tlow = split(terms)
    eighth = W32 // q
    for z in range(q):
        for p in range(q):
            cols = grad_agg[p * W32 : (p + 1) * W32, z * B : (z + 1) * B]
            out_ref[z * q + p, 0:W32, :] = cols.astype(BF)
            first = p * W32 + z * eighth
            piece = [thigh[first : first + eighth], tlow[first : first + eighth]]
            out_ref[z * q + p, W32:, :] = jnp.concatenate(piece, axis=0).astype(BF)


def owner_kernel(q, got_ref, out_ref):
    total = got_ref[0].astype(F32)
    for r in range(1, got_ref.shape[0]):
        total = total + got_ref[r].astype(F32)
    eighth = W32 // q
    high, low = split(total[W32 : W32 + eighth] + total[W32 + eighth :])
    sent = jnp.concatenate([total[:W32], high, low], axis=0).astype(BF)
    for d in range(out_ref.shape[0]):
        out_ref[d] = sent


def merge_kernel(q, got_ref, out_ref):
    count = got_ref.shape[0]
    nh = count // q
    eighth = W32 // q
    blocks = got_ref[:, 0:W32, :].reshape(count * W32, B)
    rows = []
    for z in range(q):
        total = got_ref[z * nh, W32:, :].astype(F32)
        for h in range(1, nh):
            total = total + got_ref[z * nh + h, W32:, :].astype(F32)
        rows.append(total[:eighth] + total[eighth:])
    terms = jnp.concatenate(rows, axis=0).astype(BF)
    for d in range(out_ref.shape[0]):
        out_ref[d, 0 : count * W32, :] = blocks
        out_ref[d, count * W32 :, :] = terms


def features_kernel(q, nx, nh, nl, rows_ref, live_ref, got_ref, tiles_ref, gft_ref, gw_ref):
    slots = tiles_ref.shape[1]
    blocks = []
    for s in range(slots):
        row = rows_ref[0, s]
        plane, column = lax.div(row, nx * nh * nl), lax.rem(row, nx * nh * nl)
        line, place = lax.div(column, nh * nl), lax.rem(column, nh * nl)
        near = line * nl + lax.rem(place, nl)
        first = pl.multiple_of((plane * nh + lax.div(place, nl)) * W32, W32)
        live = live_ref[0, s].astype(F32)
        blocks.append((got_ref[near, pl.ds(first, W32), :].astype(F32) * live).astype(BF))
    total = nn(jnp.concatenate(blocks, axis=1), tiles_ref[0].reshape(slots * B, B))
    gft_ref[...] = total.astype(BF)
    first = q * nh * W32
    terms = got_ref[:, first:, :].astype(F32)
    gw_ref[...] = jnp.sum(terms, axis=0) * (1.0 / math.sqrt(q * nx * nh * nl * B))


def on_device(features, weight, tiles, tile_rows, tile_live, pos_partner, neg_partner):
    q, nx = lax.axis_size("zh"), lax.axis_size("x")
    nh, nl = lax.axis_size("yh"), lax.axis_size("yl")
    xy, near, far = nx * nh * nl, nx * nl, q * nh
    axes = (REP, "zh", COLUMN)
    place = jnp.stack([lax.axis_index(axis) for axis in axes]).astype(jnp.int32)
    shape = jax.ShapeDtypeStruct
    slots = 2 * pos_partner.shape[1]
    groups = xy * W32 // B
    pos_t, neg_t = pos_partner.T, neg_partner.T

    sent = call(
        functools.partial(products_kernel, nx, nh, nl),
        [SMEM, SMEM, VMEM, VMEM],
        shape((near, far, W32, B), BF),
        [pltpu.VMEM((near, far, W32, B), F32)],
        params=pltpu.CompilerParams(vmem_limit_bytes=60 * 1024 * 1024),
    )(tile_rows, tile_live, features.T, tiles)
    near_recv = lax.all_to_all(sent.reshape(near, far * W32, B), NEAR, 0, 0, tiled=True)

    near_sum = call(near_kernel, [VMEM], shape((far * W32, B), BF))(near_recv)
    recv = lax.all_to_all(near_sum.reshape(far, W32, B), FAR, 0, 0, tiled=True)
    own = call(
        aggregate_kernel, [SMEM] + [VMEM] * 3, shape((q * q, W32 + slots, B), BF)
    )(place, recv, pos_t, neg_t)
    blocks = lax.all_to_all(own, ("zh",) + REP, 0, 0, tiled=True)

    nodes, agg, emb_t, slab_part = call(
        functools.partial(embed_kernel, q),
        [SMEM] + [VMEM] * 4,
        (
            shape((q * B, F), BF),
            shape((q, F, B), BF),
            shape((W32, B), BF),
            shape((xy, W32 + slots, B), BF),
        ),
        [pltpu.VMEM((q, F, B), BF)],
    )(place, blocks, weight, pos_t, neg_t)
    slab = lax.all_to_all(slab_part, COLUMN, 0, 0, tiled=True)
    cpos, ctot = call(
        functools.partial(direct_kernel, q, xy, slots),
        [SMEM, VMEM],
        (shape((groups, q * B, B), BF), shape((groups, q * B, B), BF)),
        [pltpu.VMEM((B, B), F32), pltpu.VMEM((slots, B, B), F32)],
        flops=100000000,
    )(place, blocks)

    pieces = call(
        functools.partial(decoder_kernel, q, xy, slots),
        [SMEM] + [VMEM] * 6,
        shape((q * q, W32 + 2 * W32 // q, B), BF),
        [
            pltpu.VMEM((groups, q * B, B), F32),
            pltpu.VMEM((groups, q * B, B), BF),
        ],
    )(place, slab, nodes, agg, weight, cpos, ctot)
    mine = lax.all_to_all(pieces, ("zh",) + REP, 0, 0, tiled=True)

    height = pieces.shape[1]
    far_part = call(functools.partial(owner_kernel, q), [VMEM], shape((far, height, B), BF))(mine)
    lines = lax.all_to_all(far_part, FAR, 0, 0, tiled=True)
    near_part = call(
        functools.partial(merge_kernel, q), [VMEM], shape((near, (far + 1) * W32, B), BF)
    )(lines)
    every = lax.all_to_all(near_part, NEAR, 0, 0, tiled=True)

    gf_t, grad_weight = call(
        functools.partial(features_kernel, q, nx, nh, nl),
        [SMEM, SMEM, VMEM, VMEM],
        (shape((W32, B), BF), shape((W32, F), F32)),
    )(tile_rows, tile_live, every, tiles)
    return (emb_t.T, grad_weight, gf_t.T)


def sharded(mesh):
    return jax.shard_map(
        on_device,
        mesh=mesh,
        in_specs=(
            P(ROWS, REP),
            P(),
            P(ROWS, None, None, None),
            P(ROWS, None),
            P(ROWS, None),
            P(ROWS, None),
            P(ROWS, None),
        ),
        out_specs=(P(ROWS, REP), P(REP, None), P(ROWS, REP)),
        check_vma=False,
    )


def solution(mesh):
    rows = mesh.shape["rows"]
    parts = mesh.devices.reshape(4, 4, rows // 32, 2, 2, 2)
    return sharded(Mesh(parts, ROWS + REP))
```

```python
import functools
import math

import jax
import jax.numpy as jnp
from jax import lax
from jax.experimental import pallas as pl
from jax.experimental.pallas import tpu as pltpu
from jax.sharding import Mesh, PartitionSpec as P

BF = jnp.bfloat16
F32 = jnp.float32
B = 128
F = 128
W32 = 32
NEAR = ("x", "yl")
FAR = ("zh", "yh")
COLUMN = ("x", "yh", "yl")
ROWS = ("zh",) + COLUMN
REP = ("zl", "core")
PARAMS = pltpu.CompilerParams(vmem_limit_bytes=40 * 1024 * 1024)
VMEM = pl.BlockSpec(memory_space=pltpu.VMEM)
SMEM = pl.BlockSpec(memory_space=pltpu.SMEM)


def tn(a, b):
    return lax.dot_general(a, b, (((0,), (0,)), ((), ())), preferred_element_type=F32)


def nt(a, b):
    return lax.dot_general(a, b, (((1,), (1,)), ((), ())), preferred_element_type=F32)


def nn(a, b):
    return lax.dot_general(a, b, (((1,), (0,)), ((), ())), preferred_element_type=F32)


def call(body, in_specs, out_shape, scratch=(), flops=1000000, nbytes=1000000, params=PARAMS):
    multi = isinstance(out_shape, (tuple, list))
    return pl.pallas_call(
        body,
        out_shape=out_shape,
        in_specs=in_specs,
        out_specs=[VMEM] * len(out_shape) if multi else VMEM,
        scratch_shapes=list(scratch),
        compiler_params=params,
        cost_estimate=pl.CostEstimate(flops=flops, bytes_accessed=nbytes, transcendentals=0),
    )


def split(value):
    high = value.astype(BF).astype(F32)
    return high, value - high


def products_kernel(nx, nh, nl, rows_ref, live_ref, feat_ref, tiles_ref, out_ref, acc):
    out_ref[...] = jnp.zeros_like(out_ref)
    slots = tiles_ref.shape[1]
    places = []
    for s in range(slots):
        row = rows_ref[0, s]
        plane, column = lax.div(row, nx * nh * nl), lax.rem(row, nx * nh * nl)
        line, place = lax.div(column, nh * nl), lax.rem(column, nh * nl)
        near = line * nl + lax.rem(place, nl)
        places.append((near, plane * nh + lax.div(place, nl)))
        acc[places[s]] = jnp.zeros((W32, B), F32)
    for s in range(slots):
        acc[places[s]] += nt(feat_ref[...], tiles_ref[0, s]) * live_ref[0, s].astype(F32)
    for s in range(slots):
        out_ref[places[s]] = acc[places[s]].astype(BF)


def near_kernel(recv_ref, out_ref):
    total = recv_ref[0].astype(F32)
    for r in range(1, recv_ref.shape[0]):
        total = total + recv_ref[r].astype(F32)
    out_ref[...] = total.astype(BF)


def aggregate_kernel(place_ref, recv_ref, pos_ref, neg_ref, out_ref):
    total = recv_ref[0].astype(F32)
    for r in range(1, recv_ref.shape[0]):
        total = total + recv_ref[r].astype(F32)
    total = total.astype(BF)
    ids = jnp.concatenate([pos_ref[...], neg_ref[...]], axis=0)
    block = lax.shift_right_logical(ids, 7)
    table = jnp.where(lax.rem(place_ref[0], 2) == 0, block, ids - block * B).astype(F32).astype(BF)
    for d in range(out_ref.shape[0]):
        out_ref[d, 0:W32, :] = total
        out_ref[d, W32:, :] = table


def embed_kernel(
    q, place_ref, got_ref, w_ref, pos_ref, neg_ref, nodes_ref, agg_ref, embt_ref, send_ref, et_s
):
    part, plane, column = place_ref[0], place_ref[1], place_ref[2]
    for b in range(q):
        for p in range(q):
            agg_ref[b, p * W32 : (p + 1) * W32, :] = got_ref[b * q + p, 0:W32, :]
        et = tn(w_ref[...], agg_ref[b])
        et_s[b] = et.astype(BF)
        nodes_ref[b * B : (b + 1) * B, :] = et.T.astype(BF)
    embt_ref[...] = et_s[plane, pl.ds(pl.multiple_of(part * W32, W32), W32), :]
    nodes = nodes_ref[pl.ds(pl.multiple_of(plane * B + part * W32, W32), W32), :]
    ids = jnp.concatenate([pos_ref[...], neg_ref[...]], axis=0)
    block = lax.shift_right_logical(ids, 7)
    lane = lax.broadcasted_iota(jnp.int32, ids.shape, 1)
    first = part * W32
    mine = (lane >= first) & (lane < first + W32)
    blocks = jnp.where(mine, block, 0).astype(F32)
    places = jnp.where(mine, ids - block * B, 0).astype(F32)
    quarters = B // W32
    turn = lax.rem(lax.rem(column, quarters) - part + quarters, quarters) * W32
    partners = pltpu.roll(blocks + pltpu.roll(places, B // 2, 1), turn, 1).astype(BF)
    for d in range(send_ref.shape[0]):
        send_ref[d, 0:W32, :] = nodes
        send_ref[d, W32:, :] = partners


def direct_kernel(q, xy, slots, place_ref, got_ref, cpos_ref, ctot_ref, want_s, wide_s):
    part, plane = place_ref[0], place_ref[1]
    pk = slots // 2
    lane = lax.broadcasted_iota(jnp.int32, (B, B), 1).astype(F32)
    first_block = (plane * xy).astype(F32)
    first_place = (part * W32).astype(F32)
    for d in range(q):
        piece = got_ref[d * q, W32:, :].astype(F32) - first_block
        place = got_ref[d * q + 1, W32:, :].astype(F32) - first_place
        inside = (piece >= 0.0) & (piece < float(xy)) & (place >= 0.0) & (place < float(W32))
        want = jnp.where(inside, piece * W32 + place, -1.0)
        want_s[...] = jnp.concatenate([want, jnp.zeros((B - slots, B), F32)], axis=0).T
        for k in range(slots):
            wide_s[k] = jnp.broadcast_to(want_s[:, k : k + 1], (B, B))

        def step(g, carry):
            at = lane + (g * B).astype(F32)
            cpos = jnp.zeros((B, B), F32)
            cneg = jnp.zeros((B, B), F32)
            for k in range(pk):
                cpos = jnp.where(wide_s[k] == at, cpos + 1.0, cpos)
                cneg = jnp.where(wide_s[pk + k] == at, cneg + 1.0, cneg)
            cpos_ref[g, d * B : (d + 1) * B, :] = cpos.astype(BF)
            ctot_ref[g, d * B : (d + 1) * B, :] = (cpos + cneg).astype(BF)
            return carry

        lax.fori_loop(0, cpos_ref.shape[0], step, 0)


def decoder_kernel(
    q, xy, slots, place_ref, got_ref, en_ref, agg_ref, w_ref, cpos_ref, ctot_ref,
    out_ref, logit_s, coef_s,
):
    pk = slots // 2
    column = place_ref[2]
    quarters = B // W32
    groups = got_ref.shape[0] // quarters
    tile = 16
    sub = [
        (lax.broadcasted_iota(jnp.int32, (tile, B), 0) + i * tile).astype(F32).astype(BF)
        for i in range(B // tile)
    ]
    en = en_ref[...]
    for g in range(groups):
        em = got_ref[g * quarters : (g + 1) * quarters, 0:W32, :].reshape(B, F)
        logit_s[g] = nt(en, em)
    quarter = lax.div(lax.broadcasted_iota(jnp.int32, (slots, B), 1), W32)
    half = 0.5 / math.sqrt(F)
    one, zero = jnp.ones((tile, B), BF), jnp.zeros((tile, B), BF)

    def step(g, carry):
        theirs = jnp.zeros((slots, B), F32)
        places = jnp.zeros((slots, B), F32)
        for j in range(quarters):
            table = got_ref[g * quarters + j, W32:, :].astype(F32)
            theirs = jnp.where(quarter == j, table, theirs)
            places = jnp.where(quarter == (j + quarters // 2) % quarters, table, places)
        places = pltpu.roll(places, B // 2, 1)
        for d in range(q):
            block = d * xy + column
            code = jnp.where(theirs == block.astype(F32), places, -1.0)
            wide = [
                jnp.broadcast_to(code[k : k + 1], (tile, B)).astype(BF) for k in range(slots)
            ]
            both, ineg = [], []
            for i in range(B // tile):
                cp, cn = zero, zero
                for k in range(pk):
                    cp = jnp.where(wide[k] == sub[i], cp + one, cp)
                    cn = jnp.where(wide[pk + k] == sub[i], cn + one, cn)
                both.append(cp)
                ineg.append(cp + cn)
            rows = slice(d * B, (d + 1) * B)
            cpos = (cpos_ref[g, rows, :] + jnp.concatenate(both, axis=0)).astype(F32)
            ctot = (ctot_ref[g, rows, :] + jnp.concatenate(ineg, axis=0)).astype(F32)
            sig = 0.5 * jnp.tanh(logit_s[g, rows, :] * half) + 0.5
            coef_s[g, rows, :] = (ctot * sig - cpos).astype(BF)
        return carry

    lax.fori_loop(0, groups, step, 0)
    grad = jnp.zeros((q * B, F), F32)
    for g in range(groups):
        em = got_ref[g * quarters : (g + 1) * quarters, 0:W32, :].reshape(B, F)
        grad = grad + nn(coef_s[g], em)
    grad = (grad * (1.0 / pk)).astype(BF)
    grad_agg = nt(w_ref[...], grad)
    terms = jnp.zeros((F, F), F32)
    for d in range(q):
        rows = slice(d * B, (d + 1) * B)
        terms = terms + nn(agg_ref[d], grad[rows])
    thigh, tlow = split(terms)
    eighth = W32 // q
    for z in range(q):
        for p in range(q):
            cols = grad_agg[p * W32 : (p + 1) * W32, z * B : (z + 1) * B]
            out_ref[z * q + p, 0:W32, :] = cols.astype(BF)
            first = p * W32 + z * eighth
            piece = [thigh[first : first + eighth], tlow[first : first + eighth]]
            out_ref[z * q + p, W32:, :] = jnp.concatenate(piece, axis=0).astype(BF)


def owner_kernel(q, got_ref, out_ref):
    total = got_ref[0].astype(F32)
    for r in range(1, got_ref.shape[0]):
        total = total + got_ref[r].astype(F32)
    eighth = W32 // q
    high, low = split(total[W32 : W32 + eighth] + total[W32 + eighth :])
    sent = jnp.concatenate([total[:W32], high, low], axis=0).astype(BF)
    for d in range(out_ref.shape[0]):
        out_ref[d] = sent


def merge_kernel(q, got_ref, out_ref):
    count = got_ref.shape[0]
    nh = count // q
    eighth = W32 // q
    blocks = got_ref[:, 0:W32, :].reshape(count * W32, B)
    rows = []
    for z in range(q):
        total = got_ref[z * nh, W32:, :].astype(F32)
        for h in range(1, nh):
            total = total + got_ref[z * nh + h, W32:, :].astype(F32)
        rows.append(total[:eighth] + total[eighth:])
    terms = jnp.concatenate(rows, axis=0).astype(BF)
    for d in range(out_ref.shape[0]):
        out_ref[d, 0 : count * W32, :] = blocks
        out_ref[d, count * W32 :, :] = terms


def features_kernel(q, nx, nh, nl, rows_ref, live_ref, got_ref, tiles_ref, gft_ref, gw_ref):
    slots = tiles_ref.shape[1]
    blocks = []
    for s in range(slots):
        row = rows_ref[0, s]
        plane, column = lax.div(row, nx * nh * nl), lax.rem(row, nx * nh * nl)
        line, place = lax.div(column, nh * nl), lax.rem(column, nh * nl)
        near = line * nl + lax.rem(place, nl)
        first = pl.multiple_of((plane * nh + lax.div(place, nl)) * W32, W32)
        live = live_ref[0, s].astype(F32)
        blocks.append((got_ref[near, pl.ds(first, W32), :].astype(F32) * live).astype(BF))
    total = nn(jnp.concatenate(blocks, axis=1), tiles_ref[0].reshape(slots * B, B))
    gft_ref[...] = total.astype(BF)
    first = q * nh * W32
    terms = got_ref[:, first:, :].astype(F32)
    gw_ref[...] = jnp.sum(terms, axis=0) * (1.0 / math.sqrt(q * nx * nh * nl * B))


def on_device(features, weight, tiles, tile_rows, tile_live, pos_partner, neg_partner):
    q, nx = lax.axis_size("zh"), lax.axis_size("x")
    nh, nl = lax.axis_size("yh"), lax.axis_size("yl")
    xy, near, far = nx * nh * nl, nx * nl, q * nh
    axes = (REP, "zh", COLUMN)
    place = jnp.stack([lax.axis_index(axis) for axis in axes]).astype(jnp.int32)
    shape = jax.ShapeDtypeStruct
    slots = 2 * pos_partner.shape[1]
    groups = xy * W32 // B
    pos_t, neg_t = pos_partner.T, neg_partner.T

    sent = call(
        functools.partial(products_kernel, nx, nh, nl),
        [SMEM, SMEM, VMEM, VMEM],
        shape((near, far, W32, B), BF),
        [pltpu.VMEM((near, far, W32, B), F32)],
        params=pltpu.CompilerParams(vmem_limit_bytes=60 * 1024 * 1024),
    )(tile_rows, tile_live, features.T, tiles)
    near_recv = lax.all_to_all(sent.reshape(near, far * W32, B), NEAR, 0, 0, tiled=True)

    near_sum = call(near_kernel, [VMEM], shape((far * W32, B), BF))(near_recv)
    recv = lax.all_to_all(near_sum.reshape(far, W32, B), FAR, 0, 0, tiled=True)
    own = call(
        aggregate_kernel, [SMEM] + [VMEM] * 3, shape((q * q, W32 + slots, B), BF)
    )(place, recv, pos_t, neg_t)
    blocks = lax.all_to_all(own, ("zh",) + REP, 0, 0, tiled=True)

    nodes, agg, emb_t, slab_part = call(
        functools.partial(embed_kernel, q),
        [SMEM] + [VMEM] * 4,
        (
            shape((q * B, F), BF),
            shape((q, F, B), BF),
            shape((W32, B), BF),
            shape((xy, W32 + slots, B), BF),
        ),
        [pltpu.VMEM((q, F, B), BF)],
    )(place, blocks, weight, pos_t, neg_t)
    slab = lax.all_to_all(slab_part, COLUMN, 0, 0, tiled=True)
    cpos, ctot = call(
        functools.partial(direct_kernel, q, xy, slots),
        [SMEM, VMEM],
        (shape((groups, q * B, B), BF), shape((groups, q * B, B), BF)),
        [pltpu.VMEM((B, B), F32), pltpu.VMEM((slots, B, B), F32)],
        flops=100000000,
    )(place, blocks)

    pieces = call(
        functools.partial(decoder_kernel, q, xy, slots),
        [SMEM] + [VMEM] * 6,
        shape((q * q, W32 + 2 * W32 // q, B), BF),
        [
            pltpu.VMEM((groups, q * B, B), F32),
            pltpu.VMEM((groups, q * B, B), BF),
        ],
    )(place, slab, nodes, agg, weight, cpos, ctot)
    mine = lax.all_to_all(pieces, ("zh",) + REP, 0, 0, tiled=True)

    height = pieces.shape[1]
    far_part = call(functools.partial(owner_kernel, q), [VMEM], shape((far, height, B), BF))(mine)
    lines = lax.all_to_all(far_part, FAR, 0, 0, tiled=True)
    near_part = call(
        functools.partial(merge_kernel, q), [VMEM], shape((near, (far + 1) * W32, B), BF)
    )(lines)
    every = lax.all_to_all(near_part, NEAR, 0, 0, tiled=True)

    gf_t, grad_weight = call(
        functools.partial(features_kernel, q, nx, nh, nl),
        [SMEM, SMEM, VMEM, VMEM],
        (shape((W32, B), BF), shape((W32, F), F32)),
    )(tile_rows, tile_live, every, tiles)
    return (emb_t.T, grad_weight, gf_t.T)


def sharded(mesh):
    return jax.shard_map(
        on_device,
        mesh=mesh,
        in_specs=(
            P(ROWS, REP),
            P(),
            P(ROWS, None, None, None),
            P(ROWS, None),
            P(ROWS, None),
            P(ROWS, None),
            P(ROWS, None),
        ),
        out_specs=(P(ROWS, REP), P(REP, None), P(ROWS, REP)),
        check_vma=False,
    )


def solution(mesh):
    rows = mesh.shape["rows"]
    parts = mesh.devices.reshape(4, 4, rows // 32, 2, 2, 2)
    return sharded(Mesh(parts, ROWS + REP))
```
